32 devices in a mesh: groups: 2 (over x), col: 16 (over z, y, core).
Axes of the slice: x: 2, y: 2, z: 4, core: 2. Of those that a mesh axis runs over, the one named last changes fastest.
Arguments:
- features: bfloat16 [32, 8, 8192], P(('groups', 'col')), parts along dimension 0
- zone_ids: int32 [32], P(('groups', 'col')), parts along dimension 0, may hold values from 0 to 7, as said below
- golden_owner: int32 [16], P('groups'), parts along dimension 0, may hold values from 0 to 15, as said below
- defect_mask: int32 [32, 8, 128], P(('groups', 'col')), parts along dimension 0, may hold values 0 or 1
- kernels: bfloat16 [2, 576, 64], replicated, may hold values from -0.25 to 0.25
Outputs:
- score: float32 [32, 8, 128], P(('groups', 'col')), parts along dimension 0
The draws below stay inside these ranges and needn't reach their ends.
There are 2 independent parts, one for each index of `groups`. The reference program is written for one: setup_inputs(seed, part) draws one part's arguments, and reference() takes and returns one part's arrays. A program takes and returns all parts, laid end to end along the dimension named above; an argument that names none is the same for every part. Nothing has to cross between parts.
Inputs may be any that keep to these rules, and one draw needn't show every extreme that they name: `zone_ids`: every zone holds at least one die. golden_owner[z] is a die of zone z.
All inputs are finite; a program needn't handle non-finite values. No bound on the sum of `defect_mask` on one device may be relied on, other than what follows from the above.
Results may differ from the reference program's by a relative error of at most 0.0039.
Values may be sent and summed in bfloat16 or wider, within the bound.
No kernel may reach another device: no remote copies, remote signals or barrier semaphores. Data moves between devices by JAX's collectives and lax.ppermute only.
A program may use at most 64 MiB of HBM per device.

```python
import jax
import jax.numpy as jnp
from jax import lax

C = 64
H = 8
W = 128
SHIFT = 6
BOX = 5
Z = 8
DIES = 16


def layout(key):
    base = jax.random.fold_in(key, 101)
    key_order = jax.random.fold_in(base, 1)
    key_map = jax.random.fold_in(base, 2)
    key_pick = jax.random.fold_in(base, 3)
    order = jax.random.permutation(key_order, DIES).astype(jnp.int32)
    zone_map = jax.random.permutation(key_map, Z).astype(jnp.int32)
    picks = jax.random.randint(key_pick, (3, DIES), 0, Z)
    common = zone_map[jnp.min(picks, axis=0)]
    slots = jnp.arange(DIES, dtype=jnp.int32)
    assign = jnp.where(slots < Z, slots, common).astype(jnp.int32)
    zones = jnp.zeros((DIES,), jnp.int32).at[order].set(assign)
    owners = order[0:Z]
    return (zones, owners)


def draw_zone_ids(key, part):
    zones, owners = layout(key)
    return zones


def draw_golden_owner(key, part):
    zones, owners = layout(key)
    return owners


def draw_features(key, part):
    zones, owners = layout(key)
    base = jax.random.fold_in(key, 202)
    key_rough = jax.random.fold_in(base, 1)
    key_noise = jax.random.fold_in(base, 2)
    key_rank = jax.random.fold_in(base, 3)
    key_spot = jax.random.fold_in(base, 4)
    key_size = jax.random.fold_in(base, 5)
    key_sign = jax.random.fold_in(base, 7)
    key_magn = jax.random.fold_in(base, 8)
    side = 2 * SHIFT + 1
    others = min(side, 2 * H - 1) * min(side, 2 * W - 1) - 1
    rank = jax.random.permutation(key_rank, Z).astype(jnp.float32)
    share = 0.24 + 0.09 * rank / (Z - 1)
    rough_scale = jnp.sqrt(share / (1.0 - share))
    leak = 1.2 * others * jnp.exp(-32.0 * share)
    amplify = 1.0 / (leak * rough_scale)
    signs = jnp.where(jax.random.bernoulli(key_sign, 0.5, (Z, C)), 1.0, -1.0).astype(jnp.float32)
    magnitude = jax.random.uniform(key_magn, (Z, C), jnp.float32, 0.8, 1.2)
    rough = jax.random.normal(key_rough, (Z, H, W, C), jnp.float32)
    noise = jax.random.normal(key_noise, (DIES, H, W, C), jnp.float32)
    zone_scale = jnp.ones((Z,), jnp.float32)
    pattern = (signs * magnitude)[:, None, None, :] + rough_scale[:, None, None, None] * rough
    pattern = pattern * amplify[:, None, None, None]
    tiles = jnp.take(pattern, zones, axis=0)
    spots = (jax.random.uniform(key_spot, (DIES, H, W, 1)) < 0.02).astype(jnp.float32)
    spots = 4.0 * spots * jax.random.normal(key_size, (DIES, H, W, C), jnp.float32)
    whole = (tiles + noise + spots) * jnp.take(zone_scale, zones)[:, None, None, None]
    return whole.reshape(DIES, H, W * C).astype(jnp.bfloat16)


def with_ends(values, stream_key, smallest, high):
    spot = [jax.random.randint(jax.random.fold_in(stream_key, axis), (), 0, length) for axis, length in enumerate(values.shape)]
    widest = values.shape.index(max(values.shape))
    next_to = spot[:widest] + [(spot[widest] + 1) % values.shape[widest]] + spot[widest + 1:]
    return values.at[tuple(spot)].set(smallest).at[tuple(next_to)].set(high)


def scatter_about(key, shape, deviation, limit, kind=jnp.bfloat16):
    return jnp.clip(deviation * jax.random.normal(key, shape, jnp.float32), -limit, limit).astype(kind)


def setup_inputs(seed: int = 0, part: int = 0) -> dict:
    keys = jax.random.split(jax.random.key(seed), 6)
    part_splits = jax.random.split(jax.random.fold_in(keys[5], part), 6)
    return {
        "features": draw_features(jax.random.fold_in(jax.random.fold_in(keys[5], part), 71), part),
        "zone_ids": draw_zone_ids(jax.random.fold_in(jax.random.fold_in(keys[5], part), 71), part),
        "golden_owner": draw_golden_owner(jax.random.fold_in(jax.random.fold_in(keys[5], part), 71), part),
        "defect_mask": with_ends((jax.random.randint(part_splits[3], (DIES, H, W), 0, 2) < 1).astype(jnp.int32), jax.random.fold_in(part_splits[3], 1), 0, 1),
        "kernels": scatter_about(keys[4], (2, 9 * C, C), (9 * C) ** -0.5, 0.25),
    }


def box_sum(plane):
    rows = plane.shape[0]
    cols = plane.shape[1]
    reach = BOX // 2
    padded = jnp.pad(plane, ((reach, reach), (reach, reach)))
    across = padded[0:rows]
    for offset in range(1, BOX):
        across = across + padded[offset:offset + rows]
    total = across[:, 0:cols]
    for offset in range(1, BOX):
        total = total + across[:, offset:offset + cols]
    return total

def align_golden(test_tile, golden_tile):
    height, width, chans = test_tile.shape
    side = 2 * SHIFT + 1
    test_f = test_tile.astype(jnp.float32)
    padded = jnp.pad(golden_tile.astype(jnp.float32), ((SHIFT, SHIFT), (SHIFT, SHIFT), (0, 0)))
    self_energy = box_sum(lax.optimization_barrier(jnp.sum(test_f * test_f, axis=-1)))

    def shifted(index):
        row_off = (index // side).astype(jnp.int32)
        col_off = (index % side).astype(jnp.int32)
        return lax.dynamic_slice(padded, (row_off, col_off, jnp.int32(0)), (height, width, chans))

    def logit(index):
        moved = shifted(index)
        cross = box_sum(lax.optimization_barrier(jnp.sum(test_f * moved, axis=-1)))
        other = box_sum(lax.optimization_barrier(jnp.sum(moved * moved, axis=-1)))
        return 32.0 * cross / jnp.sqrt(self_energy * other + 1e-05)
    shift_ids = jnp.arange(side * side, dtype=jnp.int32)
    logits = lax.map(logit, shift_ids)
    expo = jnp.exp(logits)
    weights = expo / lax.optimization_barrier(jnp.sum(expo, axis=0))

    def accumulate(total, pair):
        index, weight = pair
        return (total + weight[:, :, None] * shifted(index), None)
    aligned, _ = lax.scan(accumulate, jnp.zeros((height, width, chans), jnp.float32), (shift_ids, weights))
    return aligned

def conv_three(tile, kernel):
    height, width, chans = tile.shape
    padded = jnp.pad(tile, ((1, 1), (1, 1), (0, 0)))
    total = jnp.zeros((height * width, kernel.shape[1]), jnp.float32)
    for tap in range(9):
        row_off = tap // 3
        col_off = tap % 3
        window = padded[row_off:row_off + height, col_off:col_off + width].reshape(height * width, chans)
        total = total + jnp.dot(window, kernel[tap * chans:(tap + 1) * chans], preferred_element_type=jnp.float32)
    return total.reshape(height, width, kernel.shape[1])

def inspect_die(test_tile, golden_tile, kernels):
    aligned = align_golden(test_tile, golden_tile)
    residual = (test_tile.astype(jnp.float32) - aligned).astype(jnp.bfloat16)
    hidden = jax.nn.relu(conv_three(residual, kernels[0])).astype(jnp.bfloat16)
    refined = residual.astype(jnp.float32) + conv_three(hidden, kernels[1])
    return lax.optimization_barrier(jnp.mean(refined * refined, axis=-1))

def reference(features, zone_ids, golden_owner, defect_mask, kernels):

    def one_die(die):
        test_tile = features[die].reshape(H, W, C)
        golden_tile = features[golden_owner[zone_ids[die]]].reshape(H, W, C)
        return inspect_die(test_tile, golden_tile, kernels)
    energy = lax.map(one_die, jnp.arange(DIES, dtype=jnp.int32))
    masked = defect_mask.astype(jnp.float32)
    die_sum = lax.optimization_barrier(jnp.sum(energy * masked, axis=(1, 2)))
    die_count = lax.optimization_barrier(jnp.sum(masked, axis=(1, 2)))
    onehot = (zone_ids[:, None] == jnp.arange(Z, dtype=jnp.int32)[None, :]).astype(jnp.float32)
    zone_sum = lax.optimization_barrier(jnp.sum(onehot * die_sum[:, None], axis=0))
    zone_count = lax.optimization_barrier(jnp.sum(onehot * die_count[:, None], axis=0))
    zone_mean = zone_sum / jnp.maximum(zone_count, 1.0)
    mine = lax.optimization_barrier(jnp.sum(onehot * zone_mean[None, :], axis=1))
    return energy / (mine[:, None, None] + 0.01)
```

```python
import functools

import jax
import jax.numpy as jnp
from jax import lax
from jax.experimental import pallas as pl
from jax.experimental.pallas import tpu as pltpu
from jax.sharding import PartitionSpec as P

C = 64
SHIFT = 6
BOX = 5
Z = 8
SIDE = 2 * SHIFT + 1
REACH = BOX // 2
HALO = SHIFT + REACH + 2
ROWS = 8
SLOT = 16
TOP = (SLOT - ROWS) // 2
LANES = 128
LOG2E = 1.4426950408889634
F32 = jnp.float32
BF16 = jnp.bfloat16


def iota(shape, dim):
    return lax.broadcasted_iota(jnp.int32, shape, dim)


def pack_kernel(chips, w, zone_ref, feat_ref, mask_ref, out_ref):
    width = mask_ref.shape[2]
    half = (w + 2 * HALO) // 2
    zone = zone_ref[0].astype(F32)
    mask = mask_ref[0].astype(F32)
    lane = iota((ROWS, LANES), 1)
    for p in range(chips):
        for t in range(half // 2):
            parts = []
            for part in range(2):
                col = p * w - HALO + part * half + 2 * t
                if 0 <= col < width:
                    parts.append(feat_ref[0, :, col * C : (col + 2) * C].astype(F32))
                else:
                    parts.append(jnp.zeros((ROWS, LANES), F32))
            out_ref[p, :, t * LANES : (t + 1) * LANES] = jnp.concatenate(parts, 0).astype(BF16)
        here = pltpu.roll(mask, (width - p * w) % width, 1) if p else mask
        here = jnp.where(lane < w, here, 0.0)
        last = jnp.concatenate([here, jnp.full((ROWS, LANES), 1.0, F32) * zone], 0)
        out_ref[p, :, half // 2 * LANES :] = last.astype(BF16)


def main_kernel(
    chips, w, me_ref, owner_ref, own_ref, other_ref, kern_ref, out_ref,
    pad_ref, test_ref, gold_ref, goldc_ref, goldsq_ref, self_ref, res_ref, hid_ref,
):
    cols = w + 2 * HALO
    half = cols // 2
    raw = w + 4 + 2 * REACH
    outs = w + 4
    me = me_ref[0]
    chip = me // 2
    core = me % 2
    not_first = jnp.where(chip == 0, 0.0, 1.0).astype(F32)
    not_last = jnp.where(chip == chips - 1, 0.0, 1.0).astype(F32)

    lane8 = iota((ROWS, LANES), 1)
    sub8 = iota((ROWS, LANES), 0)
    low8 = lane8 < C
    low16 = iota((SLOT, LANES), 1) < C
    ones = jnp.ones((LANES, LANES), BF16)
    ones2 = jnp.ones((2 * LANES, LANES), BF16)

    twice = (iota((C, LANES), 1) % C == iota((C, LANES), 0)).astype(BF16)
    weights = []
    for conv in range(2):
        doubled = jnp.dot(kern_ref[conv], twice, preferred_element_type=F32).astype(BF16)
        by_col = []
        for dx in range(3):
            taps = [doubled[(3 * dy + dx) * C : (3 * dy + dx + 1) * C] for dy in range(3)]
            by_col.append(jnp.concatenate(taps + [jnp.zeros((C, LANES), BF16)], 0))
        weights.append(jnp.concatenate(by_col, 1))

    spread_r = iota((LANES, 2 * LANES), 0)
    spread_c = iota((LANES, 2 * LANES), 1)
    spread = ((spread_c // LANES == spread_r // C) & (spread_c % C == spread_r % C)).astype(BF16)
    zero8 = jnp.zeros((ROWS, LANES), F32)
    for which, src in enumerate((own_ref, other_ref)):

        def unpack(i, carry, src=src, base=which * chips):
            for g in range(cols + 1):
                pad_ref[base + i, g * SLOT : g * SLOT + ROWS, :] = zero8
            for t in range(half // 2):
                both = jnp.dot(src[i, :, t * LANES : (t + 1) * LANES], spread, preferred_element_type=F32)
                for part in range(2):
                    for odd in range(2):
                        row = (part * half + 2 * t + odd) * SLOT + ROWS
                        pad_ref[base + i, row : row + ROWS, :] = both[
                            part * ROWS : (part + 1) * ROWS, odd * LANES : (odd + 1) * LANES
                        ]
            return carry

        lax.fori_loop(0, chips, unpack, 0)

    for ref, count in ((self_ref, outs), (res_ref, outs), (hid_ref, w + 2)):
        for i in range(count + 1):
            ref[i * SLOT : i * SLOT + ROWS, :] = zero8
    goldsq_ref[cols * SLOT :, :] = jnp.zeros((goldsq_ref.shape[0] - cols * SLOT, LANES), BF16)

    lane_w = iota((ROWS, 2 * LANES), 1)
    sub_w = iota((ROWS, 2 * LANES), 0)
    valid = []
    for k in range(4):
        b = lane_w // SLOT - k
        a = lane_w % SLOT - TOP - sub_w
        valid.append((b >= 0) & (b < SIDE) & (jnp.abs(a) <= SHIFT))
    outside = jnp.maximum(SHIFT - TOP - sub8, 0) + jnp.maximum(sub8 + SHIFT - (SLOT - TOP - 1), 0)
    outside = (outside * SIDE).astype(F32)

    lanes_g = goldsq_ref.shape[0]
    sub_g = iota((ROWS, lanes_g), 0)

    def split_square(values, low):
        square = values * values
        high = square.astype(BF16).astype(F32)
        return jnp.where(low, high, square - high).astype(BF16)

    def one_die(i, zones):
        tail = own_ref[i, :, half // 2 * LANES :].astype(F32)
        mask = tail[:ROWS]
        zone = tail[ROWS, 0].astype(jnp.int32)
        owner = owner_ref[zone]
        gold = owner // 2 + jnp.where(owner % 2 == core, 0, chips)

        for g in range(cols):
            rows = [pad_ref[gold, g * SLOT + TOP + dy : g * SLOT + TOP + dy + SLOT, :] for dy in range(-2, 3)]
            at = slice(g * SLOT, (g + 1) * SLOT)
            gold_ref[at, 0:LANES] = jnp.where(low16, rows[0], rows[1]).astype(BF16)
            gold_ref[at, LANES : 2 * LANES] = jnp.where(low16, rows[2], rows[3]).astype(BF16)
            gold_ref[at, 2 * LANES :] = rows[4].astype(BF16)
            goldc_ref[at, :] = rows[2].astype(BF16)
            goldsq_ref[at, :] = split_square(rows[2], low16)
        squares = []
        for r in range(0, raw, 2):
            tiles = [[], [], []]
            centre = []
            for q in (r, r + 1):
                base = (q + HALO - REACH - 2) * SLOT + ROWS
                rows = [pad_ref[i, base + dy : base + dy + ROWS, :] for dy in range(-2, 3)]
                tiles[0].append(jnp.where(low8, rows[0], rows[1]))
                tiles[1].append(jnp.where(low8, rows[2], rows[3]))
                tiles[2].append(jnp.where(low8, rows[4], 0.0))
                centre.append(rows[2])
            at = slice(r * ROWS, (r + 2) * ROWS)
            for t in range(3):
                test_ref[at, t * LANES : (t + 1) * LANES] = jnp.concatenate(tiles[t], 0).astype(BF16)
            squares.append(split_square(jnp.concatenate(centre, 0), low16))

        energy = jnp.dot(jnp.concatenate(squares, 0), ones, preferred_element_type=F32)
        energy = [energy[r * ROWS : (r + 1) * ROWS] for r in range(raw)]
        for l in range(outs):
            self_ref[l * SLOT + ROWS : (l + 1) * SLOT, :] = sum(energy[l + 1 : l + BOX], energy[l])
        self_box = []
        for l in range(outs):
            base = l * SLOT + ROWS
            rows = [self_ref[base + dy : base + dy + ROWS, :] for dy in range(-2, 3)]
            self_box.append(sum(rows[1:], rows[0]))

        e = lax.dot_general(
            jnp.ones((SLOT, LANES), BF16), goldsq_ref[...], (((1,), (1,)), ((), ())), preferred_element_type=F32
        )[:ROWS]
        down = e
        for dy in (-2, -1, 1, 2):
            inside = (sub_g + dy >= 0) & (sub_g + dy < ROWS)
            down = down + jnp.where(inside, pltpu.roll(e, (-dy) % lanes_g, 1), 0.0)
        moved = [down] + [pltpu.roll(down, lanes_g - SLOT * d, 1) for d in range(1, BOX)]
        whole = sum(moved[1:], moved[0])
        edge = {
            2: moved[2] + moved[3] + moved[4] + not_first * (moved[0] + moved[1]),
            3: moved[1] + moved[2] + moved[3] + moved[4] + not_first * moved[0],
            w: moved[0] + moved[1] + moved[2] + moved[3] + not_last * moved[4],
            w + 1: moved[0] + moved[1] + moved[2] + not_last * (moved[3] + moved[4]),
        }
        whole_by = (whole, pltpu.roll(whole, lanes_g - C, 1))
        edge = {l: pltpu.roll(v, lanes_g - C, 1) if (l // 4) % 2 else v for l, v in edge.items()}

        sheared = []
        for j in range(raw // 4):
            block = lax.dot_general(
                test_ref[4 * j * ROWS : 4 * (j + 1) * ROWS, :],
                gold_ref[4 * j * SLOT : (4 * j + 16) * SLOT, :],
                (((1,), (1,)), ((), ())),
                preferred_element_type=F32,
            )
            for k in range(4):
                row = block[k * ROWS : (k + 1) * ROWS]
                sheared.append(pltpu.roll(row, 2 * LANES - k * SLOT, 1) if k else row)
        pairs = [sheared[r] + sheared[r + 1] for r in range(raw - 1)]
        res = []
        for m in range(outs // 4):
            chosen = []
            for k in range(4):
                l = 4 * m + k
                cross = pairs[l] + pairs[l + 2] + sheared[l + 4]
                cross = pltpu.roll(cross, k * SLOT, 1) if k else cross
                src = edge.get(l, whole_by[m % 2])
                at = (m - m % 2) * C
                scale = lax.rsqrt(jnp.concatenate([self_box[l]] * 2, 1) * src[:, at : at + 2 * LANES] + 1e-05)
                expo = jnp.exp2((32.0 * LOG2E) * cross * scale)
                chosen.append(jnp.where(valid[k], expo, 0.0))
            weight = jnp.concatenate(chosen, 0).astype(BF16)
            at = (4 * m + 2) * SLOT
            numer = jnp.dot(weight, goldc_ref[at : at + 16 * SLOT, :], preferred_element_type=F32)
            denom = jnp.dot(weight, ones2, preferred_element_type=F32)
            for k in range(4):
                l = 4 * m + k
                at = slice(k * ROWS, (k + 1) * ROWS)
                base = (l + HALO - 2) * SLOT + ROWS
                value = pad_ref[i, base : base + ROWS, :] - numer[at] / (denom[at] + outside)
                if l < 2:
                    value = value * not_first
                if l >= w + 2:
                    value = value * not_last
                value = value.astype(BF16).astype(F32)
                res.append(value)
                res_ref[l * SLOT + ROWS : (l + 1) * SLOT, :] = value

        def convolve(ref, count, weight):
            first, second = [], []
            for l in range(count):
                base = l * SLOT + ROWS
                first.append(jnp.where(low8, ref[base - 1 : base - 1 + ROWS, :], ref[base : base + ROWS, :]))
                second.append(ref[base + 1 : base + 1 + ROWS, :])
            rows = jnp.concatenate([jnp.concatenate(first, 0), jnp.concatenate(second, 0)], 1).astype(BF16)
            full = jnp.dot(rows, weight, preferred_element_type=F32)
            full = [full[l * ROWS : (l + 1) * ROWS] for l in range(count)]
            return [
                full[x][:, :LANES] + full[x + 1][:, LANES : 2 * LANES] + full[x + 2][:, 2 * LANES :]
                for x in range(count - 2)
            ]

        for h, value in enumerate(convolve(res_ref, outs, weights[0])):
            value = jnp.maximum(value, 0.0).astype(BF16).astype(F32)
            if h == 0:
                value = value * not_first
            if h == w + 1:
                value = value * not_last
            hid_ref[h * SLOT + ROWS : (h + 1) * SLOT, :] = value
        found = jnp.zeros((ROWS, LANES), F32)
        for x, value in enumerate(convolve(hid_ref, w + 2, weights[1])):
            refined = res[x + 2] + value
            mean = jnp.sum(refined * refined, axis=1, keepdims=True) * (1.0 / LANES)
            found = jnp.where(lane8 == x, mean, found)

        out_ref[2 * i + core] = found
        out_ref[2 * i + 1 - core] = jnp.zeros((ROWS, LANES), F32)
        mask = jnp.where(lane8 < w, mask, 0.0)
        total = jnp.sum(jnp.sum(found * mask, axis=1, keepdims=True), axis=0, keepdims=True)
        count = jnp.sum(jnp.sum(mask, axis=1, keepdims=True), axis=0, keepdims=True)
        here = sub8 == zone
        zones = zones + jnp.where(here & (lane8 == w), total, 0.0)
        return zones + jnp.where(here & (lane8 == w + 1), count, 0.0)

    zones = lax.fori_loop(0, chips, one_die, jnp.zeros((ROWS, LANES), F32))
    for d in range(2 * chips):
        out_ref[d] = out_ref[d] + zones


def score_kernel(chips, w, zone_ref, back_ref, out_ref):
    lane = iota((ROWS, LANES), 1)
    sub = iota((ROWS, LANES), 0)
    total = back_ref[0]
    for d in range(1, 2 * chips):
        total = total + back_ref[d]
    mine = jnp.where(sub == zone_ref[0], total, 0.0)
    zone_sum = jnp.sum(jnp.sum(jnp.where(lane == w, mine, 0.0), axis=1, keepdims=True), axis=0, keepdims=True)
    zone_count = jnp.sum(jnp.sum(jnp.where(lane == w + 1, mine, 0.0), axis=1, keepdims=True), axis=0, keepdims=True)
    zone_mean = zone_sum / jnp.maximum(zone_count, 1.0)
    energy = jnp.zeros((ROWS, LANES), F32)
    for p in range(chips):
        strip = back_ref[2 * p] + back_ref[2 * p + 1]
        strip = pltpu.roll(strip, p * w, 1) if p else strip
        energy = jnp.where((lane >= p * w) & (lane < (p + 1) * w), strip, energy)
    out_ref[0] = energy / (zone_mean + 0.01)


def body(n, features, zone_ids, golden_owner, defect_mask, kernels):
    chips = n // 2
    w = defect_mask.shape[2] // chips
    cols = w + 2 * HALO
    raw = w + 4 + 2 * REACH
    outs = w + 4
    half = cols // 2
    length = half * C + LANES
    smem = pl.BlockSpec(memory_space=pltpu.SMEM)
    vmem = pl.BlockSpec(memory_space=pltpu.VMEM)
    params = pltpu.CompilerParams(vmem_limit_bytes=48 * 2**20)

    packed = pl.pallas_call(
        functools.partial(pack_kernel, chips, w),
        out_shape=jax.ShapeDtypeStruct((chips, 2 * ROWS, length), BF16),
        in_specs=[smem, vmem, vmem],
        out_specs=vmem,
        compiler_params=params,
    )(zone_ids, features, defect_mask)
    groups = [[2 * p + c for p in range(chips)] for c in range(2)]
    own = lax.all_to_all(packed, "col", 0, 0, axis_index_groups=groups, tiled=True)
    other = lax.ppermute(own, "col", [(d, d ^ 1) for d in range(n)])
    me = lax.axis_index("col").astype(jnp.int32).reshape(1)
    lanes_g = -(-cols * SLOT // LANES) * LANES
    partial = pl.pallas_call(
        functools.partial(main_kernel, chips, w),
        out_shape=jax.ShapeDtypeStruct((n, ROWS, LANES), F32),
        in_specs=[smem, smem, vmem, vmem, vmem],
        out_specs=vmem,
        scratch_shapes=[
            pltpu.VMEM((n, cols * SLOT + ROWS, LANES), F32),
            pltpu.VMEM((raw * ROWS, 3 * LANES), BF16),
            pltpu.VMEM((cols * SLOT, 3 * LANES), BF16),
            pltpu.VMEM((cols * SLOT, LANES), BF16),
            pltpu.VMEM((lanes_g, LANES), BF16),
            pltpu.VMEM((outs * SLOT + ROWS, LANES), F32),
            pltpu.VMEM((outs * SLOT + ROWS, LANES), F32),
            pltpu.VMEM(((w + 2) * SLOT + ROWS, LANES), F32),
        ],
        compiler_params=params,
    )(me, golden_owner, own, other, kernels)
    back = lax.all_to_all(partial, "col", 0, 0, tiled=True)
    return pl.pallas_call(
        functools.partial(score_kernel, chips, w),
        out_shape=jax.ShapeDtypeStruct(defect_mask.shape, F32),
        in_specs=[smem, vmem],
        out_specs=vmem,
        compiler_params=params,
    )(zone_ids, back)


def solution(mesh):
    split = P(("groups", "col"), None, None)
    return jax.shard_map(
        functools.partial(body, mesh.shape["col"]),
        mesh=mesh,
        in_specs=(split, P(("groups", "col")), P("groups"), split, P()),
        out_specs=split,
        check_vma=False,
    )
```

```python
import functools

import jax
import jax.numpy as jnp
from jax import lax
from jax.experimental import pallas as pl
from jax.experimental.pallas import tpu as pltpu
from jax.sharding import PartitionSpec as P

C = 64
SHIFT = 6
BOX = 5
Z = 8
SIDE = 2 * SHIFT + 1
REACH = BOX // 2
HALO = SHIFT + REACH + 2
ROWS = 8
SLOT = 16
TOP = (SLOT - ROWS) // 2
LANES = 128
PAIR = 4
LOG2E = 1.4426950408889634
F32 = jnp.float32
BF16 = jnp.bfloat16


def iota(shape, dim):
    return lax.broadcasted_iota(jnp.int32, shape, dim)


def pack_kernel(chips, w, zone_ref, feat_ref, mask_ref, out_ref):
    width = mask_ref.shape[2]
    half = (w + 2 * HALO) // 2
    zone = zone_ref[0].astype(F32)
    mask = mask_ref[0].astype(F32)
    lane = iota((ROWS, LANES), 1)
    for p in range(chips):
        for t in range(half // 2):
            parts = []
            for part in range(2):
                col = p * w - HALO + part * half + 2 * t
                if 0 <= col < width:
                    parts.append(feat_ref[0, :, col * C : (col + 2) * C].astype(F32))
                else:
                    parts.append(jnp.zeros((ROWS, LANES), F32))
            out_ref[p, :, t * LANES : (t + 1) * LANES] = jnp.concatenate(parts, 0).astype(BF16)
        here = pltpu.roll(mask, (width - p * w) % width, 1) if p else mask
        here = jnp.where(lane < w, here, 0.0)
        last = jnp.concatenate([here, jnp.full((ROWS, LANES), 1.0, F32) * zone], 0)
        out_ref[p, :, half // 2 * LANES :] = last.astype(BF16)


def main_kernel(
    chips, w, me_ref, owner_ref, own_ref, other_ref, kern_ref, out_ref, res_ref, hid_ref, *scratch
):
    cols = w + 2 * HALO
    half = cols // 2
    raw = w + 4 + 2 * REACH
    outs = w + 4
    me = me_ref[0]
    chip = me // 2
    core = me % 2
    not_first = jnp.where(chip == 0, 0.0, 1.0).astype(F32)
    not_last = jnp.where(chip == chips - 1, 0.0, 1.0).astype(F32)

    lane8 = iota((ROWS, LANES), 1)
    sub8 = iota((ROWS, LANES), 0)
    low8 = lane8 < C
    low16 = iota((SLOT, LANES), 1) < C
    ones = jnp.ones((LANES, LANES), BF16)
    ones2 = jnp.ones((2 * LANES, LANES), BF16)
    zero8 = jnp.zeros((ROWS, LANES), F32)

    twice = (iota((C, LANES), 1) % C == iota((C, LANES), 0)).astype(BF16)
    weights = []
    for conv in range(2):
        doubled = jnp.dot(kern_ref[conv], twice, preferred_element_type=F32).astype(BF16)
        by_col = []
        for dx in range(3):
            taps = [doubled[(3 * dy + dx) * C : (3 * dy + dx + 1) * C] for dy in range(3)]
            by_col.append(jnp.concatenate(taps + [jnp.zeros((C, LANES), BF16)], 0))
        weights.append(jnp.concatenate(by_col, 1))

    zones, golds = [], []
    for i in range(chips):
        zone = own_ref[i, :, half // 2 * LANES :].astype(F32)[ROWS, 0].astype(jnp.int32)
        zones.append(zone)
        golds.append(owner_ref[zone])

    def pick(values, step, u):
        found = values[u]
        for i in range(1, chips // PAIR):
            found = jnp.where(step == i, values[PAIR * i + u], found)
        return found

    for u in range(PAIR):
        gpad_ref, tpad_ref, _, _, _, goldsq_ref, self_ref = scratch[7 * u : 7 * u + 7]
        for ref, count in ((gpad_ref, cols), (tpad_ref, raw), (self_ref, outs)):
            for i in range(count + 1):
                ref[i * SLOT : i * SLOT + ROWS, :] = zero8
        goldsq_ref[cols * SLOT :, :] = jnp.zeros((goldsq_ref.shape[0] - cols * SLOT, LANES), BF16)

    lane_w = iota((ROWS, 2 * LANES), 1)
    sub_w = iota((ROWS, 2 * LANES), 0)
    valid = []
    for k in range(4):
        b = lane_w // SLOT - k
        a = lane_w % SLOT - TOP - sub_w
        valid.append((b >= 0) & (b < SIDE) & (jnp.abs(a) <= SHIFT))
    outside = jnp.maximum(SHIFT - TOP - sub8, 0) + jnp.maximum(sub8 + SHIFT - (SLOT - TOP - 1), 0)
    outside = (outside * SIDE).astype(F32)

    lanes_g = scratch[5].shape[0]
    sub_g = iota((ROWS, lanes_g), 0)

    def split_square(values, low):
        square = values * values
        high = square.astype(BF16).astype(F32)
        return jnp.where(low, high, square - high).astype(BF16)

    def spread(tile):
        tile = tile.astype(F32)
        found = []
        for part in range(2):
            here = tile[part * ROWS : (part + 1) * ROWS]
            turned = pltpu.roll(here, C, 1)
            found.append((jnp.where(low8, here, turned), jnp.where(low8, turned, here)))
        return found

    def align(i, owner, gpad_ref, tpad_ref, test_ref, gold_ref, goldc_ref, goldsq_ref, self_ref):
        mine = owner % 2 == core
        for t in range(half // 2):
            at = slice(t * LANES, (t + 1) * LANES)
            tile = jnp.where(mine, own_ref[owner // 2, :, at], other_ref[owner // 2, :, at])
            for part, both in enumerate(spread(tile)):
                for odd, value in enumerate(both):
                    row = (part * half + 2 * t + odd) * SLOT + ROWS
                    gpad_ref[row : row + ROWS, :] = value
            for part, both in enumerate(spread(own_ref[i, :, at])):
                for odd, value in enumerate(both):
                    r = part * half + 2 * t + odd - (HALO - REACH - 2)
                    if 0 <= r < raw:
                        tpad_ref[r * SLOT + ROWS : (r + 1) * SLOT, :] = value
        for g in range(cols):
            rows = [gpad_ref[g * SLOT + TOP + dy : g * SLOT + TOP + dy + SLOT, :] for dy in range(-2, 3)]
            at = slice(g * SLOT, (g + 1) * SLOT)
            gold_ref[at, 0:LANES] = jnp.where(low16, rows[0], rows[1]).astype(BF16)
            gold_ref[at, LANES : 2 * LANES] = jnp.where(low16, rows[2], rows[3]).astype(BF16)
            gold_ref[at, 2 * LANES :] = rows[4].astype(BF16)
            goldc_ref[at, :] = rows[2].astype(BF16)
            goldsq_ref[at, :] = split_square(rows[2], low16)
        squares = []
        for r in range(0, raw, 2):
            tiles = [[], [], []]
            centre = []
            for q in (r, r + 1):
                base = q * SLOT + ROWS
                rows = [tpad_ref[base + dy : base + dy + ROWS, :] for dy in range(-2, 3)]
                tiles[0].append(jnp.where(low8, rows[0], rows[1]))
                tiles[1].append(jnp.where(low8, rows[2], rows[3]))
                tiles[2].append(jnp.where(low8, rows[4], 0.0))
                centre.append(rows[2])
            at = slice(r * ROWS, (r + 2) * ROWS)
            for t in range(3):
                test_ref[at, t * LANES : (t + 1) * LANES] = jnp.concatenate(tiles[t], 0).astype(BF16)
            squares.append(split_square(jnp.concatenate(centre, 0), low16))

        energy = jnp.dot(jnp.concatenate(squares, 0), ones, preferred_element_type=F32)
        energy = [energy[r * ROWS : (r + 1) * ROWS] for r in range(raw)]
        for l in range(outs):
            self_ref[l * SLOT + ROWS : (l + 1) * SLOT, :] = sum(energy[l + 1 : l + BOX], energy[l])
        self_box = []
        for l in range(outs):
            base = l * SLOT + ROWS
            rows = [self_ref[base + dy : base + dy + ROWS, :] for dy in range(-2, 3)]
            self_box.append(sum(rows[1:], rows[0]))

        e = lax.dot_general(
            jnp.ones((SLOT, LANES), BF16), goldsq_ref[...], (((1,), (1,)), ((), ())), preferred_element_type=F32
        )[:ROWS]
        down = e
        for dy in (-2, -1, 1, 2):
            inside = (sub_g + dy >= 0) & (sub_g + dy < ROWS)
            down = down + jnp.where(inside, pltpu.roll(e, (-dy) % lanes_g, 1), 0.0)
        moved = [down] + [pltpu.roll(down, lanes_g - SLOT * d, 1) for d in range(1, BOX)]
        whole = sum(moved[1:], moved[0])
        edge = {
            2: moved[2] + moved[3] + moved[4] + not_first * (moved[0] + moved[1]),
            3: moved[1] + moved[2] + moved[3] + moved[4] + not_first * moved[0],
            w: moved[0] + moved[1] + moved[2] + moved[3] + not_last * moved[4],
            w + 1: moved[0] + moved[1] + moved[2] + not_last * (moved[3] + moved[4]),
        }
        whole_by = (whole, pltpu.roll(whole, lanes_g - C, 1))
        edge = {l: pltpu.roll(v, lanes_g - C, 1) if (l // 4) % 2 else v for l, v in edge.items()}

        sheared = []
        for j in range(raw // 4):
            block = lax.dot_general(
                test_ref[4 * j * ROWS : 4 * (j + 1) * ROWS, :],
                gold_ref[4 * j * SLOT : (4 * j + 16) * SLOT, :],
                (((1,), (1,)), ((), ())),
                preferred_element_type=F32,
            )
            for k in range(4):
                row = block[k * ROWS : (k + 1) * ROWS]
                sheared.append(pltpu.roll(row, 2 * LANES - k * SLOT, 1) if k else row)
        pairs = [sheared[r] + sheared[r + 1] for r in range(raw - 1)]
        for m in range(outs // 4):
            chosen = []
            for k in range(4):
                l = 4 * m + k
                cross = pairs[l] + pairs[l + 2] + sheared[l + 4]
                cross = pltpu.roll(cross, k * SLOT, 1) if k else cross
                src = edge.get(l, whole_by[m % 2])
                at = (m - m % 2) * C
                scale = lax.rsqrt(jnp.concatenate([self_box[l]] * 2, 1) * src[:, at : at + 2 * LANES] + 1e-05)
                expo = jnp.exp2((32.0 * LOG2E) * cross * scale)
                chosen.append(jnp.where(valid[k], expo, 0.0))
            weight = jnp.concatenate(chosen, 0).astype(BF16)
            at = (4 * m + 2) * SLOT
            numer = jnp.dot(weight, goldc_ref[at : at + 16 * SLOT, :], preferred_element_type=F32)
            denom = jnp.dot(weight, ones2, preferred_element_type=F32)
            for k in range(4):
                l = 4 * m + k
                at = slice(k * ROWS, (k + 1) * ROWS)
                base = (l + REACH) * SLOT + ROWS
                value = tpad_ref[base : base + ROWS, :] - numer[at] / (denom[at] + outside)
                if l < 2:
                    value = value * not_first
                if l >= w + 2:
                    value = value * not_last
                res_ref[i, l * SLOT + ROWS : (l + 1) * SLOT, :] = value.astype(BF16).astype(F32)

    def align_step(step, carry):
        for u in range(PAIR):
            i = PAIR * step + u
            for x in range(outs + 1):
                res_ref[i, x * SLOT : x * SLOT + ROWS, :] = zero8
            align(i, pick(golds, step, u), *scratch[7 * u : 7 * u + 7])
        return carry

    lax.fori_loop(0, chips // PAIR, align_step, 0)

    def convolve(read, count, weight):
        first, second = [], []
        for l in range(count):
            base = l * SLOT + ROWS
            first.append(jnp.where(low8, read(base - 1), read(base)))
            second.append(read(base + 1))
        rows = jnp.concatenate([jnp.concatenate(first, 0), jnp.concatenate(second, 0)], 1).astype(BF16)
        full = jnp.dot(rows, weight, preferred_element_type=F32)
        full = [full[l * ROWS : (l + 1) * ROWS] for l in range(count)]
        return [
            full[x][:, :LANES] + full[x + 1][:, LANES : 2 * LANES] + full[x + 2][:, 2 * LANES :]
            for x in range(count - 2)
        ]

    def hidden_step(step, carry):
        for u in range(PAIR):
            i = PAIR * step + u
            for x in range(w + 3):
                hid_ref[i, x * SLOT : x * SLOT + ROWS, :] = zero8
            for h, value in enumerate(convolve(lambda at: res_ref[i, at : at + ROWS, :], outs, weights[0])):
                value = jnp.maximum(value, 0.0).astype(BF16).astype(F32)
                if h == 0:
                    value = value * not_first
                if h == w + 1:
                    value = value * not_last
                hid_ref[i, h * SLOT + ROWS : (h + 1) * SLOT, :] = value
        return carry

    lax.fori_loop(0, chips // PAIR, hidden_step, 0)

    def energy_step(step, sums):
        for u in range(PAIR):
            i = PAIR * step + u
            found = zero8
            for x, value in enumerate(convolve(lambda at: hid_ref[i, at : at + ROWS, :], w + 2, weights[1])):
                base = (x + 2) * SLOT + ROWS
                refined = res_ref[i, base : base + ROWS, :] + value
                mean = jnp.sum(refined * refined, axis=1, keepdims=True) * (1.0 / LANES)
                found = jnp.where(lane8 == x, mean, found)
            out_ref[2 * i + core] = found
            out_ref[2 * i + 1 - core] = zero8
            mask = own_ref[i, :, half // 2 * LANES :].astype(F32)[:ROWS]
            mask = jnp.where(lane8 < w, mask, 0.0)
            total = jnp.sum(jnp.sum(found * mask, axis=0, keepdims=True), axis=1, keepdims=True)
            count = jnp.sum(jnp.sum(mask, axis=0, keepdims=True), axis=1, keepdims=True)
            here = sub8 == pick(zones, step, u)
            sums = sums + jnp.where(here & (lane8 == w), total, 0.0) + jnp.where(here & (lane8 == w + 1), count, 0.0)
        return sums

    sums = lax.fori_loop(0, chips // PAIR, energy_step, zero8)
    for d in range(2 * chips):
        out_ref[d] = out_ref[d] + sums


def scratches(n, w):
    cols, raw, outs = w + 2 * HALO, w + 4 + 2 * REACH, w + 4
    lanes_g = -(-cols * SLOT // LANES) * LANES
    one = [
        pltpu.VMEM((cols * SLOT + ROWS, LANES), F32),
        pltpu.VMEM((raw * SLOT + ROWS, LANES), F32),
        pltpu.VMEM((raw * ROWS, 3 * LANES), BF16),
        pltpu.VMEM((cols * SLOT, 3 * LANES), BF16),
        pltpu.VMEM((cols * SLOT, LANES), BF16),
        pltpu.VMEM((lanes_g, LANES), BF16),
        pltpu.VMEM((outs * SLOT + ROWS, LANES), F32),
    ]
    return [
        pltpu.VMEM((n // 2, outs * SLOT + ROWS, LANES), F32),
        pltpu.VMEM((n // 2, (w + 2) * SLOT + ROWS, LANES), F32),
    ] + one * PAIR


def score_kernel(chips, w, zone_ref, back_ref, out_ref):
    lane = iota((ROWS, LANES), 1)
    sub = iota((ROWS, LANES), 0)
    total = back_ref[0]
    for d in range(1, 2 * chips):
        total = total + back_ref[d]
    mine = jnp.where(sub == zone_ref[0], total, 0.0)
    zone_sum = jnp.sum(jnp.sum(jnp.where(lane == w, mine, 0.0), axis=1, keepdims=True), axis=0, keepdims=True)
    zone_count = jnp.sum(jnp.sum(jnp.where(lane == w + 1, mine, 0.0), axis=1, keepdims=True), axis=0, keepdims=True)
    zone_mean = zone_sum / jnp.maximum(zone_count, 1.0)
    energy = jnp.zeros((ROWS, LANES), F32)
    for p in range(chips):
        strip = back_ref[2 * p] + back_ref[2 * p + 1]
        strip = pltpu.roll(strip, p * w, 1) if p else strip
        energy = jnp.where((lane >= p * w) & (lane < (p + 1) * w), strip, energy)
    out_ref[0] = energy / (zone_mean + 0.01)


def body(n, features, zone_ids, golden_owner, defect_mask, kernels):
    chips = n // 2
    w = defect_mask.shape[2] // chips
    cols = w + 2 * HALO
    half = cols // 2
    length = half * C + LANES
    smem = pl.BlockSpec(memory_space=pltpu.SMEM)
    vmem = pl.BlockSpec(memory_space=pltpu.VMEM)
    params = pltpu.CompilerParams(vmem_limit_bytes=48 * 2**20)

    packed = pl.pallas_call(
        functools.partial(pack_kernel, chips, w),
        out_shape=jax.ShapeDtypeStruct((chips, 2 * ROWS, length), BF16),
        in_specs=[smem, vmem, vmem],
        out_specs=vmem,
        compiler_params=params,
    )(zone_ids, features, defect_mask)
    groups = [[2 * p + c for p in range(chips)] for c in range(2)]
    own = lax.all_to_all(packed, "col", 0, 0, axis_index_groups=groups, tiled=True)
    other = lax.ppermute(own, "col", [(d, d ^ 1) for d in range(n)])
    me = lax.axis_index("col").astype(jnp.int32).reshape(1)
    partial = pl.pallas_call(
        functools.partial(main_kernel, chips, w),
        out_shape=jax.ShapeDtypeStruct((n, ROWS, LANES), F32),
        in_specs=[smem, smem, vmem, vmem, vmem],
        out_specs=vmem,
        scratch_shapes=scratches(n, w),
        compiler_params=params,
    )(me, golden_owner, own, other, kernels)
    back = lax.all_to_all(partial, "col", 0, 0, tiled=True)
    return pl.pallas_call(
        functools.partial(score_kernel, chips, w),
        out_shape=jax.ShapeDtypeStruct(defect_mask.shape, F32),
        in_specs=[smem, vmem],
        out_specs=vmem,
        compiler_params=params,
    )(zone_ids, back)


def solution(mesh):
    split = P(("groups", "col"), None, None)
    return jax.shard_map(
        functools.partial(body, mesh.shape["col"]),
        mesh=mesh,
        in_specs=(split, P(("groups", "col")), P("groups"), split, P()),
        out_specs=split,
        check_vma=False,
    )
```

```python
import functools

import jax
import jax.numpy as jnp
from jax import lax
from jax.experimental import pallas as pl
from jax.experimental.pallas import tpu as pltpu
from jax.sharding import PartitionSpec as P

C = 64
SHIFT = 6
BOX = 5
Z = 8
SIDE = 2 * SHIFT + 1
REACH = BOX // 2
HALO = SHIFT + REACH + 2
ROWS = 8
SLOT = 16
TOP = (SLOT - ROWS) // 2
LANES = 128
GROUP = 4
FACTOR = 32.0 * 1.4426950408889634
F32 = jnp.float32
BF16 = jnp.bfloat16


def iota(shape, dim):
    return lax.broadcasted_iota(jnp.int32, shape, dim)


def pack_kernel(chips, w, feat_ref, tail_ref, out_ref):
    half = (w + 2 * HALO) // 2
    width = tail_ref.shape[1]
    mask = tail_ref[:ROWS].astype(F32)
    zone = tail_ref[ROWS:].astype(F32)
    lane = iota((ROWS, LANES), 1)
    for p in range(chips):
        for t in range(half // 2):
            parts = []
            for part in range(2):
                col = p * w - HALO + part * half + 2 * t
                if 0 <= col < width:
                    parts.append(feat_ref[0, :, col * C : (col + 2) * C].astype(F32))
                else:
                    parts.append(jnp.zeros((ROWS, LANES), F32))
            out_ref[p, :, t * LANES : (t + 1) * LANES] = jnp.concatenate(parts, 0).astype(BF16)
        here = pltpu.roll(mask, (width - p * w) % width, 1) if p else mask
        here = jnp.where(lane < w, here, 0.0)
        last = jnp.concatenate([here, zone], 0)
        out_ref[p, :, half // 2 * LANES :] = last.astype(BF16)


def split_square(values):
    square = values * values
    high = square.astype(BF16).astype(F32)
    return high, square - high


def place(values):
    row, col = iota((LANES, LANES), 0), iota((LANES, LANES), 1)
    highs, lows = zip(*(split_square(value) for value in values))
    squares = [jnp.concatenate([part.astype(BF16) for part in parts], 1) for parts in (highs, lows)]
    picks = [(col == 2 * q + row // C).astype(BF16) for q in range(len(values))]
    sums = jnp.dot(jnp.concatenate(squares, 0), jnp.concatenate(picks, 0), preferred_element_type=F32)
    rows = sums.shape[0] // 2
    return sums[:rows] + sums[rows:]


def test_kernel(chips, w, own_ref, test_ref, box_ref, wide_ref, *scratch):
    half = (w + 2 * HALO) // 2
    raw = w + 4 + 2 * REACH
    before = HALO - REACH - 2
    zero8 = jnp.zeros((ROWS, LANES), F32)
    lo, hi = slice(0, C), slice(C, LANES)

    for ref in scratch:
        for i in range(0, ref.shape[0], ROWS):
            ref[i : i + ROWS, :] = zero8
    pairs = []
    for part in range(2):
        for t in range(half // 2):
            if 0 <= part * half + 2 * t - before < raw:
                rows = slice(part * ROWS, (part + 1) * ROWS)
                pairs.append([own_ref[i, :, t * LANES : (t + 1) * LANES].astype(F32)[rows] for i in range(chips)])
    parts = [split_square(jnp.concatenate([tiles[i] for tiles in pairs], 0)) for i in range(chips)]
    squares = [jnp.concatenate([part[k].astype(BF16) for part in parts], 0) for k in range(2)]
    both = (iota((2 * LANES, 2 * LANES), 0) % LANES // C == iota((2 * LANES, 2 * LANES), 1) // LANES).astype(BF16)
    wide_ref[...] = jnp.dot(jnp.concatenate(squares, 1), both, preferred_element_type=F32)
    scale = 1.0 / FACTOR**2
    for i in range(chips):
        energy = []
        for r in range(raw):
            row = (i * (raw // 2) + r // 2) * ROWS
            energy.append(wide_ref[row : row + ROWS, r % 2 * LANES : (r % 2 + 1) * LANES])
        twos = [x + y for x, y in zip(energy, energy[1:])]
        ref = scratch[6 + i % 2]
        for l in range(w + 4):
            ref[l * SLOT + ROWS : (l + 1) * SLOT, :] = (twos[l] + twos[l + 2] + energy[l + 4]) * scale
        for l in range(w + 4):
            base = l * SLOT + ROWS
            rows = [ref[base + dy : base + dy + ROWS, :] for dy in range(-2, 3)]
            box_ref[i, l * ROWS : (l + 1) * ROWS, :] = sum(rows[1:], rows[0])

    for i in range(chips):
        refs = scratch[3 * (i % 2) : 3 * (i % 2) + 3]
        for q in range(raw // 2):
            here = pairs[q][i]
            turned = pltpu.roll(here, C, 1)
            for odd, (left, right) in enumerate(((here, turned), (turned, here))):
                top = (2 * q + odd) * SLOT + ROWS
                refs[0][top + 2 : top + 2 + ROWS, lo] = left[:, lo]
                refs[0][top + 1 : top + 1 + ROWS, hi] = right[:, hi]
                refs[1][top : top + ROWS, lo] = left[:, lo]
                refs[2][top - 1 : top - 1 + ROWS, lo] = left[:, lo]
                refs[2][top - 2 : top - 2 + ROWS, hi] = right[:, hi]
        for r in range(0, raw, 2):
            at = slice(r * ROWS, (r + 2) * ROWS)
            for t, ref in enumerate(refs):
                two = [ref[q * SLOT + ROWS : (q + 1) * SLOT, :] for q in (r, r + 1)]
                test_ref[i, at, t * LANES : (t + 1) * LANES] = jnp.concatenate(two, 0).astype(BF16)
            test_ref[i, at, 3 * LANES :] = jnp.zeros((2 * ROWS, LANES), BF16)


def main_kernel(
    chips, w, me_ref, owner_ref, own_ref, other_ref, test_ref, box_ref, kern_ref, out_ref,
    res_ref, hid_ref, g0_ref, g1_ref, g2_ref, gsq_ref, weight_ref, *scratch
):
    cols = w + 2 * HALO
    half = cols // 2
    raw = w + 4 + 2 * REACH
    outs = w + 4
    odds = half * SLOT
    chunks = -(-half // 8)
    lanes_g = chunks * LANES
    golds_ref = scratch[:4]
    kept = [scratch[4 + k * (chunks + 1) : 4 + (k + 1) * (chunks + 1)] for k in range(3)]
    me = me_ref[0]
    chip = me // 2
    core = me % 2
    not_first = jnp.where(chip == 0, 0.0, 1.0).astype(F32)
    not_last = jnp.where(chip == chips - 1, 0.0, 1.0).astype(F32)

    lane8 = iota((ROWS, LANES), 1)
    sub8 = iota((ROWS, LANES), 0)
    low8 = lane8 < C
    zero8 = jnp.zeros((ROWS, LANES), F32)
    lo = slice(0, C)
    hi = slice(C, LANES)

    twice = (iota((C, LANES), 1) % C == iota((C, LANES), 0)).astype(BF16)
    low = iota((C, LANES), 1) < C
    for conv in range(2):
        doubled = lax.dot_general(kern_ref[conv], twice, (((0,), (0,)), ((), ())), preferred_element_type=F32)
        for dy in range(3):
            for at in range(4):
                taps = [
                    doubled[(3 * dy + dx) * C : (3 * dy + dx + 1) * C] if 0 <= dx < 3 else jnp.zeros((C, LANES), F32)
                    for dx in (at, at - 1)
                ]
                row = (4 * dy + at) * C
                weight_ref[conv, row : row + C, :] = jnp.where(low, taps[0], taps[1]).astype(BF16)

    zones = [
        [ref[i, :, half // 2 * LANES :].astype(F32)[ROWS, 0].astype(jnp.int32) for i in range(chips)]
        for ref in (own_ref, other_ref)
    ]
    golds = [owner_ref[zone] for zone in zones[0]]

    for ref in (g0_ref, g1_ref, g2_ref, gsq_ref):
        for i in range(0, ref.shape[0], ROWS):
            ref[i : i + ROWS, :] = jnp.where(low8, 0.0, 1.0) if ref is g1_ref else zero8
    summing = (iota((SLOT, 4 * LANES), 1) >= 3 * LANES).astype(BF16)

    valid = []
    for k in range(4):
        a = lane8 % SLOT - TOP - sub8
        both = []
        for parity in range(2):
            b = lane8 // SLOT * 2 + parity - k
            both.append((b >= 0) & (b < SIDE) & (jnp.abs(a) <= SHIFT))
        valid.append(both)
    outside = jnp.maximum(SHIFT - TOP - sub8, 0) + jnp.maximum(sub8 + SHIFT - (SLOT - TOP - 1), 0)
    outside = (outside * SIDE).astype(F32)

    def stage(i, gold_ref):
        owner = golds[i]
        mine = owner % 2 == core
        for t in range(half // 2):
            at = slice(t * LANES, (t + 1) * LANES)
            tile = jnp.where(mine, own_ref[owner // 2, :, at], other_ref[owner // 2, :, at]).astype(F32)
            for part in range(2):
                here = tile[part * ROWS : (part + 1) * ROWS]
                turned = pltpu.roll(here, C, 1)
                for odd, (left, right) in enumerate(((here, turned), (turned, here))):
                    top = odd * odds + (part * half // 2 + t) * SLOT + TOP
                    g0_ref[top + 2 : top + 2 + ROWS, lo] = left[:, lo]
                    g0_ref[top + 1 : top + 1 + ROWS, hi] = right[:, hi]
                    g1_ref[top : top + ROWS, lo] = left[:, lo]
                    g2_ref[top - 1 : top - 1 + ROWS, lo] = left[:, lo]
                    g2_ref[top - 2 : top - 2 + ROWS, hi] = right[:, hi]
                    high, low = split_square(jnp.where(low8, left, right))
                    gsq_ref[top : top + ROWS, :] = jnp.where(low8, high, low)
            yield
        for parity in range(2):
            for g in range(half):
                at = slice(parity * odds + g * SLOT, parity * odds + (g + 1) * SLOT)
                for t, ref in enumerate((g0_ref, g1_ref, g2_ref, gsq_ref)):
                    gold_ref[at, t * LANES : (t + 1) * LANES] = ref[at, :].astype(BF16)
                if g % 6 == 5:
                    yield

    def right(value, slots):
        return pltpu.roll(value, slots * SLOT, 1) if slots else value

    def windows(gold_ref, tile, at):
        rows = [slice(p * odds + tile * SLOT, p * odds + (tile + 8) * SLOT) for p in range(2)]
        return jnp.concatenate([gold_ref[rows[0], at], gold_ref[rows[1], at]], 0)

    def first_pair(v):
        return max(0, 8 * v - SHIFT)

    def products(i, kept, gold_ref):
        energies = ([], [])
        for v in range(chunks):
            first, last = first_pair(v), min(raw // 2 - 1, 8 * v + 7)
            tiles = min(8, half - 8 * v)
            rows = [slice(p * odds + 8 * v * SLOT, p * odds + (8 * v + (tiles if tiles <= 4 else 8)) * SLOT) for p in range(2)]
            parts = [gold_ref[rows[0], :], gold_ref[rows[1], :]]
            if tiles < 4:
                parts.append(gold_ref[: (8 - 2 * tiles) * SLOT, :])
            block = lax.dot_general(
                jnp.concatenate([summing, test_ref[i, 2 * first * ROWS : 2 * (last + 1) * ROWS, :]], 0),
                jnp.concatenate(parts, 0),
                (((1,), (1,)), ((), ())),
                preferred_element_type=F32,
            )
            for p in range(2):
                at = slice(p * LANES, (p + 1) * LANES) if tiles > 4 else slice(0, LANES)
                start = 0 if tiles > 4 else p * tiles * SLOT
                here = block[:ROWS, at]
                energies[p].append(pltpu.roll(here, LANES - start, 1) if start else here)
            kept[v][...] = block[SLOT:]
            yield

        by_parity = []
        for parity in range(2):
            parts = []
            for here in energies[parity]:
                down = here
                for dy in (-2, -1, 1, 2):
                    inside = (sub8 + dy >= 0) & (sub8 + dy < ROWS)
                    down = down + jnp.where(inside, pltpu.roll(here, (-dy) % LANES, 1), 0.0)
                parts.append(down)
            by_parity.append(jnp.concatenate(parts, 1))
        even, odd = by_parity
        even1, even2 = (pltpu.roll(even, lanes_g - d * SLOT, 1) for d in (1, 2))
        odd1, odd2 = (pltpu.roll(odd, lanes_g - d * SLOT, 1) for d in (1, 2))
        def window(values, m):
            v, offset = divmod(2 * m * SLOT, LANES)
            first = values[:, v * LANES : (v + 1) * LANES]
            if not offset:
                return first
            second = values[:, (v + 1) * LANES : (v + 2) * LANES]
            return pltpu.roll(jnp.where(lane8 >= offset, first, second), LANES - offset, 1)

        for p, terms in enumerate(((even, odd, even1, odd1, even2), (odd, even1, odd1, even2, odd2))):
            a, b, c, d, e = terms
            rows = [(m, a + b + c + d + e) for m in range(outs // 4)]
            rows.append((0, c + d + e + not_first * (a + b)))
            rows.append((0, b + c + d + e + not_first * a))
            rows.append((w // 4, a + b + c + d + not_last * e))
            rows.append((w // 4, a + b + c + not_last * (d + e)))
            for row, (m, values) in enumerate(rows):
                kept[chunks][row * ROWS : (row + 1) * ROWS, p * LANES : (p + 1) * LANES] = window(values, m)
            yield

    def average(i, kept, gold_ref):
        special = {l: outs // 4 + k for k, l in enumerate((2, 3, w, w + 1))}

        def piece(r, parity, v):
            row = (r - 2 * first_pair(v)) * ROWS
            tiles = half - 8 * v
            if tiles > 4:
                return kept[v][row : row + ROWS, parity * LANES : (parity + 1) * LANES], 0
            return kept[v][row : row + ROWS, :], parity * tiles * SLOT

        def shear(r, parity, more):
            v, slots = divmod(r // 2 + more, 8)
            value, start = piece(r, parity, v)
            if slots + SHIFT - more >= 8:
                value2, start2 = piece(r, parity, v + 1)
                if start2:
                    value2 = pltpu.roll(value2, LANES - start2, 1)
                value = jnp.where(lane8 >= slots * SLOT, value, value2)
            turn = start + slots * SLOT
            return pltpu.roll(value, LANES - turn, 1) if turn else value

        def finish(m, weight):
            values = windows(gold_ref, 2 * m + 1, slice(LANES, 2 * LANES))
            total = jnp.dot(weight, values, preferred_element_type=F32)
            for k in (0, 2):
                pair = (4 * m + k) // 2
                even, odd = total[k * ROWS : (k + 1) * ROWS], total[(k + 1) * ROWS : (k + 2) * ROWS]
                numer = jnp.where(low8, even, pltpu.roll(odd, C, 1))
                denom = jnp.where(low8, pltpu.roll(even, C, 1), odd) + outside
                part, t = divmod(HALO // 2 - 1 + pair, half // 2)
                test = own_ref[i, :, t * LANES : (t + 1) * LANES].astype(F32)[part * ROWS : (part + 1) * ROWS]
                value = test - numer / denom
                if pair == 0:
                    value = value * not_first
                if pair == outs // 2 - 1:
                    value = value * not_last
                res_ref[i, pair * SLOT + ROWS : (pair + 1) * SLOT, :] = value.astype(BF16).astype(F32)

        sheared, pairs = [], []

        def extend(count):
            for r in range(len(sheared), count):
                odd = r % 2
                sheared.append((shear(r, odd, 0), shear(r, 1 - odd, odd)))
                if r:
                    pairs.append(tuple(x + y for x, y in zip(sheared[r - 1], sheared[r])))

        for m in range(outs // 4):
            extend(4 * m + 8)
            chosen = []
            for k in range(4):
                l = 4 * m + k
                cross = [pairs[l][b] + pairs[l + 2][b] + sheared[l + 4][b] for b in range(2)]
                cross = [right(cross[k % 2], (k + 1) // 2 if k % 2 else k // 2), right(cross[1 - k % 2], k // 2)]
                mine = box_ref[i, l * ROWS : (l + 1) * ROWS, :]
                row = special.get(l, m) * ROWS
                both = []
                for p in range(2):
                    other = kept[chunks][row : row + ROWS, p * LANES : (p + 1) * LANES]
                    scale = lax.rsqrt(mine * other + 1e-05 / FACTOR**2)
                    both.append(jnp.where(valid[k][p], jnp.exp2(cross[p] * scale), 0.0))
                chosen.append(jnp.concatenate(both, 1))
            weight = jnp.concatenate(chosen, 0).astype(BF16)
            if m:
                finish(m - 1, before)
            before = weight
            yield
        finish(outs // 4 - 1, before)
        yield

    for i in range(chips):
        for x in range(outs // 2 + 1):
            res_ref[i, x * SLOT : x * SLOT + ROWS, :] = zero8
        for x in range(w // 2 + 2):
            hid_ref[i, x * SLOT : x * SLOT + ROWS, :] = zero8
    def convolve(ref, count, weight, dies):
        tiles = []
        for dy in (-1, 0, 1):
            for which in range(2):
                rows = [
                    ref[i, (p + which) * SLOT + ROWS + dy : (p + which + 1) * SLOT + dy, :]
                    for i in dies
                    for p in range(count)
                ]
                tiles.append(jnp.concatenate(rows, 0).astype(BF16))
        full = jnp.dot(jnp.concatenate(tiles, 1), weight, preferred_element_type=F32)
        return [
            (i, [full[(k * count + p) * ROWS : (k * count + p + 1) * ROWS] for p in range(count)])
            for k, i in enumerate(dies)
        ]

    def finish_dies(dies):
        for i, values in convolve(res_ref, outs // 2 - 1, weight_ref[0], dies):
            for p, value in enumerate(values):
                value = jnp.maximum(value, 0.0).astype(BF16).astype(F32)
                if p == 0:
                    value = jnp.where(low8, value * not_first, value)
                if p == w // 2:
                    value = jnp.where(low8, value, value * not_last)
                hid_ref[i, p * SLOT + ROWS : (p + 1) * SLOT, :] = value
        yield
        for i, values in convolve(hid_ref, w // 2, weight_ref[1], dies):
            for p, value in enumerate(values):
                refined[p].append(res_ref[i, (p + 1) * SLOT + ROWS : (p + 2) * SLOT, :] + value)
        yield

    refined = [[] for p in range(w // 2)]
    for slot in range(chips + 4):
        running = []
        if 0 <= slot - 1 < chips:
            i = slot - 1
            running.append(products(i, kept[i % 3], golds_ref[i % 4]))
        if 0 <= slot - 3 < chips:
            i = slot - 3
            running.append(average(i, kept[i % 3], golds_ref[i % 4]))
        if slot < chips:
            running.append(stage(slot, golds_ref[slot % 4]))
        for k in range(0, chips, GROUP):
            if slot == k + GROUP - 1 + 4:
                running.append(finish_dies(range(k, k + GROUP)))
        while running:
            running = [work for work in running if next(work, running) is not running]

    energy = place([jnp.concatenate(values, 0) for values in refined]) * (1.0 / C)
    sums = zero8
    for i in range(chips):
        found = energy[i * ROWS : (i + 1) * ROWS]
        out_ref[2 * i + core] = found
        mask = own_ref[i, :, half // 2 * LANES :].astype(F32)[:ROWS]
        mask = jnp.where(lane8 < w, mask, 0.0)
        total = jnp.sum(jnp.sum(found * mask, axis=0, keepdims=True), axis=1, keepdims=True)
        count = jnp.sum(jnp.sum(mask, axis=0, keepdims=True), axis=1, keepdims=True)
        both = jnp.where(lane8 == w, total, 0.0) + jnp.where(lane8 == w + 1, count, 0.0)
        sums = sums + jnp.where(sub8 == zones[0][i], both, 0.0)
    for i in range(chips):
        for which in range(2):
            mine = jnp.sum(jnp.where(sub8 == zones[which][i], sums, 0.0), axis=0, keepdims=True)
            mine = jnp.broadcast_to(mine, (ROWS, LANES))
            if which:
                out_ref[2 * i + 1 - core] = mine
            else:
                out_ref[2 * i + core] = out_ref[2 * i + core] + mine


def score_kernel(chips, w, back_ref, out_ref):
    lane = iota((ROWS, LANES), 1)
    total = back_ref[0]
    for d in range(1, 2 * chips):
        total = total + back_ref[d]
    zone_mean = total[:, w : w + 1] / jnp.maximum(total[:, w + 1 : w + 2], 1.0)
    energy = jnp.zeros((ROWS, LANES), F32)
    for p in range(chips):
        strip = back_ref[2 * p] + back_ref[2 * p + 1]
        strip = pltpu.roll(strip, p * w, 1) if p else strip
        energy = jnp.where((lane >= p * w) & (lane < (p + 1) * w), strip, energy)
    out_ref[0] = energy / (zone_mean + 0.01)


def body(n, features, zone_ids, golden_owner, defect_mask, kernels):
    chips = n // 2
    w = defect_mask.shape[2] // chips
    cols = w + 2 * HALO
    half = cols // 2
    raw = w + 4 + 2 * REACH
    length = half * C + LANES
    smem = pl.BlockSpec(memory_space=pltpu.SMEM)
    vmem = pl.BlockSpec(memory_space=pltpu.VMEM)
    params = pltpu.CompilerParams(vmem_limit_bytes=24 * 2**20)

    zone = jnp.pad(zone_ids.reshape(1, 1), ((0, ROWS - 1), (0, defect_mask.shape[2] - 1)))
    tail = jnp.concatenate([defect_mask[0], zone], 0)
    packed = pl.pallas_call(
        functools.partial(pack_kernel, chips, w),
        out_shape=jax.ShapeDtypeStruct((chips, 2 * ROWS, length), BF16),
        in_specs=[vmem] * 2,
        out_specs=vmem,
        compiler_params=params,
    )(features, tail)
    groups = [[2 * p + c for p in range(chips)] for c in range(2)]
    own = lax.all_to_all(packed, "col", 0, 0, axis_index_groups=groups, tiled=True)
    other = lax.ppermute(own, "col", [(d, d ^ 1) for d in range(n)])
    tests = pl.pallas_call(
        functools.partial(test_kernel, chips, w),
        out_shape=[
            jax.ShapeDtypeStruct((chips, raw * ROWS, 4 * LANES), BF16),
            jax.ShapeDtypeStruct((chips, (w + 4) * ROWS, LANES), F32),
        ],
        in_specs=[vmem],
        out_specs=[vmem] * 2,
        scratch_shapes=[
            pltpu.VMEM((chips * (raw // 2) * ROWS, 2 * LANES), F32),
        ]
        + [pltpu.VMEM((raw * SLOT + ROWS, LANES), F32)] * 6
        + [pltpu.VMEM(((w + 4) * SLOT + ROWS, LANES), F32)] * 2,
        compiler_params=params,
        cost_estimate=pl.CostEstimate(flops=10**9, bytes_accessed=10**6, transcendentals=0),
    )(own)
    me = lax.axis_index("col").astype(jnp.int32).reshape(1)
    chunks = -(-half // 8)
    reach = [min(raw // 2, 8 * v + 8) - max(0, 8 * v - SHIFT) for v in range(chunks)]
    kept = [
        pltpu.VMEM((2 * reach[v] * ROWS, (2 if half - 8 * v > 4 else 1) * LANES), F32) for v in range(chunks)
    ] + [pltpu.VMEM(((w // 4 + 5) * ROWS, 2 * LANES), F32)]
    rows = half * SLOT + -(-half // 8) * LANES
    partial = pl.pallas_call(
        functools.partial(main_kernel, chips, w),
        out_shape=jax.ShapeDtypeStruct((n, ROWS, LANES), F32),
        in_specs=[smem, smem] + [vmem] * 5,
        out_specs=vmem,
        scratch_shapes=[
            pltpu.VMEM((chips, (w // 2 + 2) * SLOT + ROWS, LANES), F32),
            pltpu.VMEM((chips, (w // 2 + 1) * SLOT + ROWS, LANES), F32),
        ]
        + [pltpu.VMEM((cols * SLOT, LANES), F32)] * 4
        + [pltpu.VMEM((2, 12 * C, LANES), BF16)]
        + [pltpu.VMEM((rows, 4 * LANES), BF16)] * 4
        + kept * 3,
        compiler_params=params,
    )(me, golden_owner, own, other, *tests, jnp.swapaxes(kernels, 1, 2))
    back = lax.all_to_all(partial, "col", 0, 0, tiled=True)
    return pl.pallas_call(
        functools.partial(score_kernel, chips, w),
        out_shape=jax.ShapeDtypeStruct(defect_mask.shape, F32),
        in_specs=[vmem],
        out_specs=vmem,
        compiler_params=params,
    )(back)


def solution(mesh):
    split = P(("groups", "col"), None, None)
    return jax.shard_map(
        functools.partial(body, mesh.shape["col"]),
        mesh=mesh,
        in_specs=(split, P(("groups", "col")), P("groups"), split, P()),
        out_specs=split,
        check_vma=False,
    )
```

```python
import functools

import jax
import jax.numpy as jnp
from jax import lax
from jax.experimental import pallas as pl
from jax.experimental.pallas import tpu as pltpu
from jax.sharding import PartitionSpec as P

C = 64
SHIFT = 6
BOX = 5
Z = 8
SIDE = 2 * SHIFT + 1
REACH = BOX // 2
HALO = SHIFT + REACH + 2
ROWS = 8
SLOT = 16
TOP = (SLOT - ROWS) // 2
LANES = 128
FACTOR = 32.0 * 1.4426950408889634
F32 = jnp.float32
BF16 = jnp.bfloat16


def iota(shape, dim):
    return lax.broadcasted_iota(jnp.int32, shape, dim)


def first_kernel(out_ref):
    out_ref[...] = jnp.zeros((ROWS, LANES), F32)


def pack_kernel(chips, w, zone_ref, first_ref, feat_ref, mask_ref, out_ref):
    half = (w + 2 * HALO) // 2
    width = mask_ref.shape[2]
    mask = mask_ref[0].astype(F32)
    zone = first_ref[...] + zone_ref[0].astype(F32)
    lane = iota((ROWS, LANES), 1)
    for p in range(chips):
        for t in range(half // 2):
            parts = []
            for part in range(2):
                col = p * w - HALO + part * half + 2 * t
                if 0 <= col < width:
                    parts.append(feat_ref[0, :, col * C : (col + 2) * C].astype(F32))
                else:
                    parts.append(jnp.zeros((ROWS, LANES), F32))
            out_ref[p, :, t * LANES : (t + 1) * LANES] = jnp.concatenate(parts, 0).astype(BF16)
        here = pltpu.roll(mask, (width - p * w) % width, 1) if p else mask
        here = jnp.where(lane < w, here, 0.0)
        last = jnp.concatenate([here, zone], 0)
        out_ref[p, :, half // 2 * LANES :] = last.astype(BF16)


def split_square(values):
    square = values * values
    high = square.astype(BF16).astype(F32)
    return high, square - high


def place(values):
    row, col = iota((LANES, LANES), 0), iota((LANES, LANES), 1)
    highs, lows = zip(*(split_square(value) for value in values))
    squares = [jnp.concatenate([part.astype(BF16) for part in parts], 1) for parts in (highs, lows)]
    picks = [(col == 2 * q + row // C).astype(BF16) for q in range(len(values))]
    sums = jnp.dot(jnp.concatenate(squares, 0), jnp.concatenate(picks, 0), preferred_element_type=F32)
    rows = sums.shape[0] // 2
    return sums[:rows] + sums[rows:]


def test_kernel(chips, w, own_ref, test_ref, box_ref, wide_ref, *scratch):
    half = (w + 2 * HALO) // 2
    raw = w + 4 + 2 * REACH
    before = HALO - REACH - 2
    zero8 = jnp.zeros((ROWS, LANES), F32)
    lo, hi = slice(0, C), slice(C, LANES)

    for ref in scratch:
        for i in range(0, ref.shape[0], ROWS):
            ref[i : i + ROWS, :] = zero8
    pairs = []
    for part in range(2):
        for t in range(half // 2):
            if 0 <= part * half + 2 * t - before < raw:
                rows = slice(part * ROWS, (part + 1) * ROWS)
                pairs.append([own_ref[i, :, t * LANES : (t + 1) * LANES].astype(F32)[rows] for i in range(chips)])
    parts = [split_square(jnp.concatenate([tiles[i] for tiles in pairs], 0)) for i in range(chips)]
    squares = [jnp.concatenate([part[k].astype(BF16) for part in parts], 0) for k in range(2)]
    both = (iota((2 * LANES, 2 * LANES), 0) % LANES // C == iota((2 * LANES, 2 * LANES), 1) // LANES).astype(BF16)
    wide_ref[...] = jnp.dot(jnp.concatenate(squares, 1), both, preferred_element_type=F32)
    scale = 1.0 / FACTOR**2
    for i in range(chips):
        energy = []
        for r in range(raw):
            row = (i * (raw // 2) + r // 2) * ROWS
            energy.append(wide_ref[row : row + ROWS, r % 2 * LANES : (r % 2 + 1) * LANES])
        twos = [x + y for x, y in zip(energy, energy[1:])]
        ref = scratch[6 + i % 2]
        for l in range(w + 4):
            ref[l * SLOT + ROWS : (l + 1) * SLOT, :] = (twos[l] + twos[l + 2] + energy[l + 4]) * scale
        for l in range(w + 4):
            base = l * SLOT + ROWS
            rows = [ref[base + dy : base + dy + ROWS, :] for dy in range(-2, 3)]
            box_ref[i, l * ROWS : (l + 1) * ROWS, :] = sum(rows[1:], rows[0])

    for i in range(chips):
        refs = scratch[3 * (i % 2) : 3 * (i % 2) + 3]
        for q in range(raw // 2):
            here = pairs[q][i]
            turned = pltpu.roll(here, C, 1)
            for odd, (left, right) in enumerate(((here, turned), (turned, here))):
                top = (2 * q + odd) * SLOT + ROWS
                refs[0][top + 2 : top + 2 + ROWS, lo] = left[:, lo]
                refs[0][top + 1 : top + 1 + ROWS, hi] = right[:, hi]
                refs[1][top : top + ROWS, lo] = left[:, lo]
                refs[2][top - 1 : top - 1 + ROWS, lo] = left[:, lo]
                refs[2][top - 2 : top - 2 + ROWS, hi] = right[:, hi]
        for r in range(0, raw, 2):
            at = slice(r * ROWS, (r + 2) * ROWS)
            for t, ref in enumerate(refs):
                two = [ref[q * SLOT + ROWS : (q + 1) * SLOT, :] for q in (r, r + 1)]
                test_ref[i, at, t * LANES : (t + 1) * LANES] = jnp.concatenate(two, 0).astype(BF16)
            test_ref[i, at, 3 * LANES :] = jnp.zeros((2 * ROWS, LANES), BF16)


def weight_kernel(kern_ref, weight_ref):
    twice = (iota((C, LANES), 1) % C == iota((C, LANES), 0)).astype(BF16)
    low = iota((C, LANES), 1) < C
    for conv in range(2):
        doubled = lax.dot_general(kern_ref[conv], twice, (((0,), (0,)), ((), ())), preferred_element_type=F32)
        for dy in range(3):
            for at in range(4):
                taps = [
                    doubled[(3 * dy + dx) * C : (3 * dy + dx + 1) * C] if 0 <= dx < 3 else jnp.zeros((C, LANES), F32)
                    for dx in (at, at - 1)
                ]
                row = (4 * dy + at) * C
                weight_ref[conv, row : row + C, :] = jnp.where(low, taps[0], taps[1]).astype(BF16)


def main_kernel(
    chips, w, me_ref, owner_ref, own_ref, other_ref, test_ref, box_ref, weight_ref, out_ref,
    res_ref, hid_ref, g0_ref, g1_ref, g2_ref, gsq_ref, *scratch
):
    cols = w + 2 * HALO
    half = cols // 2
    raw = w + 4 + 2 * REACH
    outs = w + 4
    odds = half * SLOT
    chunks = -(-half // 8)
    lanes_g = chunks * LANES
    golds_ref = scratch[:4]
    kept = [scratch[4 + k * (chunks + 1) : 4 + (k + 1) * (chunks + 1)] for k in range(3)]
    me = me_ref[0]
    chip = me // 2
    core = me % 2
    not_first = jnp.where(chip == 0, 0.0, 1.0).astype(F32)
    not_last = jnp.where(chip == chips - 1, 0.0, 1.0).astype(F32)

    lane8 = iota((ROWS, LANES), 1)
    sub8 = iota((ROWS, LANES), 0)
    low8 = lane8 < C
    zero8 = jnp.zeros((ROWS, LANES), F32)
    lo = slice(0, C)
    hi = slice(C, LANES)

    zones = [
        [ref[i, :, half // 2 * LANES :].astype(F32)[ROWS, 0].astype(jnp.int32) for i in range(chips)]
        for ref in (own_ref, other_ref)
    ]
    golds = [owner_ref[zone] for zone in zones[0]]

    for ref in (g0_ref, g1_ref, g2_ref, gsq_ref):
        for i in range(0, ref.shape[0], ROWS):
            ref[i : i + ROWS, :] = jnp.where(low8, 0.0, 1.0) if ref is g1_ref else zero8
    if half % 8 > 4:
        for ref in golds_ref:
            ref[cols * SLOT :, :] = jnp.zeros((ref.shape[0] - cols * SLOT, 4 * LANES), BF16)
    summing = (iota((SLOT, 4 * LANES), 1) >= 3 * LANES).astype(BF16)

    valid = []
    for k in range(4):
        a = lane8 % SLOT - TOP - sub8
        both = []
        for parity in range(2):
            b = lane8 // SLOT * 2 + parity - k
            both.append((b >= 0) & (b < SIDE) & (jnp.abs(a) <= SHIFT))
        valid.append(both)
    outside = jnp.maximum(SHIFT - TOP - sub8, 0) + jnp.maximum(sub8 + SHIFT - (SLOT - TOP - 1), 0)
    outside = (outside * SIDE).astype(F32)

    def stage(i, gold_ref):
        owner = golds[i]
        mine = owner % 2 == core
        for t in range(half // 2):
            at = slice(t * LANES, (t + 1) * LANES)
            tile = jnp.where(mine, own_ref[owner // 2, :, at], other_ref[owner // 2, :, at]).astype(F32)
            for part in range(2):
                here = tile[part * ROWS : (part + 1) * ROWS]
                turned = pltpu.roll(here, C, 1)
                for odd, (left, right) in enumerate(((here, turned), (turned, here))):
                    top = odd * odds + (part * half // 2 + t) * SLOT + TOP
                    g0_ref[top + 2 : top + 2 + ROWS, lo] = left[:, lo]
                    g0_ref[top + 1 : top + 1 + ROWS, hi] = right[:, hi]
                    g1_ref[top : top + ROWS, lo] = left[:, lo]
                    g2_ref[top - 1 : top - 1 + ROWS, lo] = left[:, lo]
                    g2_ref[top - 2 : top - 2 + ROWS, hi] = right[:, hi]
                    high, low = split_square(jnp.where(low8, left, right))
                    gsq_ref[top : top + ROWS, :] = jnp.where(low8, high, low)
            yield
        for parity in range(2):
            for g in range(half):
                at = slice(parity * odds + g * SLOT, parity * odds + (g + 1) * SLOT)
                for t, ref in enumerate((g0_ref, g1_ref, g2_ref, gsq_ref)):
                    gold_ref[at, t * LANES : (t + 1) * LANES] = ref[at, :].astype(BF16)
                if g % 6 == 5:
                    yield

    def right(value, slots):
        return pltpu.roll(value, slots * SLOT, 1) if slots else value

    def windows(gold_ref, tile, at):
        rows = [slice(p * odds + tile * SLOT, p * odds + (tile + 8) * SLOT) for p in range(2)]
        return jnp.concatenate([gold_ref[rows[0], at], gold_ref[rows[1], at]], 0)

    def first_pair(v):
        return max(0, 8 * v - SHIFT)

    def products(i, kept, gold_ref):
        energies = ([], [])
        for v in range(chunks):
            first, last = first_pair(v), min(raw // 2 - 1, 8 * v + 7)
            tiles = min(8, half - 8 * v)
            rows = [slice(p * odds + 8 * v * SLOT, p * odds + (8 * v + (tiles if tiles <= 4 else 8)) * SLOT) for p in range(2)]
            parts = [gold_ref[rows[0], :], gold_ref[rows[1], :]]
            if tiles < 4:
                parts.append(gold_ref[: (8 - 2 * tiles) * SLOT, :])
            block = lax.dot_general(
                jnp.concatenate([summing, test_ref[i, 2 * first * ROWS : 2 * (last + 1) * ROWS, :]], 0),
                jnp.concatenate(parts, 0),
                (((1,), (1,)), ((), ())),
                preferred_element_type=F32,
            )
            for p in range(2):
                at = slice(p * LANES, (p + 1) * LANES) if tiles > 4 else slice(0, LANES)
                start = 0 if tiles > 4 else p * tiles * SLOT
                here = block[:ROWS, at]
                energies[p].append(pltpu.roll(here, LANES - start, 1) if start else here)
            kept[v][...] = block[SLOT:]
            yield

        by_parity = []
        for parity in range(2):
            parts = []
            for here in energies[parity]:
                down = here
                for dy in (-2, -1, 1, 2):
                    inside = (sub8 + dy >= 0) & (sub8 + dy < ROWS)
                    down = down + jnp.where(inside, pltpu.roll(here, (-dy) % LANES, 1), 0.0)
                parts.append(down)
            by_parity.append(jnp.concatenate(parts, 1))
        even, odd = by_parity
        even1, even2 = (pltpu.roll(even, lanes_g - d * SLOT, 1) for d in (1, 2))
        odd1, odd2 = (pltpu.roll(odd, lanes_g - d * SLOT, 1) for d in (1, 2))
        def window(values, m):
            v, offset = divmod(2 * m * SLOT, LANES)
            first = values[:, v * LANES : (v + 1) * LANES]
            if not offset:
                return first
            second = values[:, (v + 1) * LANES : (v + 2) * LANES]
            return pltpu.roll(jnp.where(lane8 >= offset, first, second), LANES - offset, 1)

        for p, terms in enumerate(((even, odd, even1, odd1, even2), (odd, even1, odd1, even2, odd2))):
            a, b, c, d, e = terms
            rows = [(m, a + b + c + d + e) for m in range(outs // 4)]
            rows.append((0, c + d + e + not_first * (a + b)))
            rows.append((0, b + c + d + e + not_first * a))
            rows.append((w // 4, a + b + c + d + not_last * e))
            rows.append((w // 4, a + b + c + not_last * (d + e)))
            for row, (m, values) in enumerate(rows):
                kept[chunks][row * ROWS : (row + 1) * ROWS, p * LANES : (p + 1) * LANES] = window(values, m)
            yield

    def average(i, kept, gold_ref):
        special = {l: outs // 4 + k for k, l in enumerate((2, 3, w, w + 1))}

        def piece(r, parity, v):
            row = (r - 2 * first_pair(v)) * ROWS
            tiles = half - 8 * v
            if tiles > 4:
                return kept[v][row : row + ROWS, parity * LANES : (parity + 1) * LANES], 0
            return kept[v][row : row + ROWS, :], parity * tiles * SLOT

        def shear(r, parity, more):
            v, slots = divmod(r // 2 + more, 8)
            value, start = piece(r, parity, v)
            if slots + SHIFT - more >= 8:
                value2, start2 = piece(r, parity, v + 1)
                if start2:
                    value2 = pltpu.roll(value2, LANES - start2, 1)
                value = jnp.where(lane8 >= slots * SLOT, value, value2)
            turn = start + slots * SLOT
            return pltpu.roll(value, LANES - turn, 1) if turn else value

        def finish(m, weight):
            values = windows(gold_ref, 2 * m + 1, slice(LANES, 2 * LANES))
            total = jnp.dot(weight, values, preferred_element_type=F32)
            for k in (0, 2):
                pair = (4 * m + k) // 2
                even, odd = total[k * ROWS : (k + 1) * ROWS], total[(k + 1) * ROWS : (k + 2) * ROWS]
                numer = jnp.where(low8, even, pltpu.roll(odd, C, 1))
                denom = jnp.where(low8, pltpu.roll(even, C, 1), odd) + outside
                part, t = divmod(HALO // 2 - 1 + pair, half // 2)
                test = own_ref[i, :, t * LANES : (t + 1) * LANES].astype(F32)[part * ROWS : (part + 1) * ROWS]
                value = test - numer / denom
                if pair == 0:
                    value = value * not_first
                if pair == outs // 2 - 1:
                    value = value * not_last
                res_ref[i, pair * SLOT + ROWS : (pair + 1) * SLOT, :] = value.astype(BF16).astype(F32)

        sheared, pairs = [], []

        def extend(count):
            for r in range(len(sheared), count):
                odd = r % 2
                sheared.append((shear(r, odd, 0), shear(r, 1 - odd, odd)))
                if r:
                    pairs.append(tuple(x + y for x, y in zip(sheared[r - 1], sheared[r])))

        for m in range(outs // 4):
            extend(4 * m + 8)
            chosen = []
            for k in range(4):
                l = 4 * m + k
                cross = [pairs[l][b] + pairs[l + 2][b] + sheared[l + 4][b] for b in range(2)]
                cross = [right(cross[k % 2], (k + 1) // 2 if k % 2 else k // 2), right(cross[1 - k % 2], k // 2)]
                mine = box_ref[i, l * ROWS : (l + 1) * ROWS, :]
                row = special.get(l, m) * ROWS
                both = []
                for p in range(2):
                    other = kept[chunks][row : row + ROWS, p * LANES : (p + 1) * LANES]
                    scale = lax.rsqrt(mine * other + 1e-05 / FACTOR**2)
                    both.append(jnp.where(valid[k][p], jnp.exp2(cross[p] * scale), 0.0))
                chosen.append(jnp.concatenate(both, 1))
            weight = jnp.concatenate(chosen, 0).astype(BF16)
            if m:
                finish(m - 1, before)
            before = weight
            yield
        finish(outs // 4 - 1, before)
        yield

    for i in range(chips):
        for x in range(outs // 2 + 1):
            res_ref[i, x * SLOT : x * SLOT + ROWS, :] = zero8
        for x in range(w // 2 + 2):
            hid_ref[i, x * SLOT : x * SLOT + ROWS, :] = zero8
    def convolve(ref, count, weight, dies):
        tiles = []
        for dy in (-1, 0, 1):
            for which in range(2):
                rows = [
                    ref[i, (p + which) * SLOT + ROWS + dy : (p + which + 1) * SLOT + dy, :]
                    for i in dies
                    for p in range(count)
                ]
                tiles.append(jnp.concatenate(rows, 0).astype(BF16))
        full = jnp.dot(jnp.concatenate(tiles, 1), weight, preferred_element_type=F32)
        return [
            (i, [full[(k * count + p) * ROWS : (k * count + p + 1) * ROWS] for p in range(count)])
            for k, i in enumerate(dies)
        ]

    def finish_dies(dies):
        for i, values in convolve(res_ref, outs // 2 - 1, weight_ref[0], dies):
            for p, value in enumerate(values):
                value = jnp.maximum(value, 0.0).astype(BF16).astype(F32)
                if p == 0:
                    value = jnp.where(low8, value * not_first, value)
                if p == w // 2:
                    value = jnp.where(low8, value, value * not_last)
                hid_ref[i, p * SLOT + ROWS : (p + 1) * SLOT, :] = value
        yield
        for i, values in convolve(hid_ref, w // 2, weight_ref[1], dies):
            for p, value in enumerate(values):
                refined[p].append(res_ref[i, (p + 1) * SLOT + ROWS : (p + 2) * SLOT, :] + value)
        yield

    refined = [[] for p in range(w // 2)]
    groups, sizes = [], [3, 3, 2] if chips == 8 else [4] * (chips // 4)
    for size in sizes:
        groups.append(range(sum(map(len, groups)), sum(map(len, groups)) + size))
    for slot in range(chips + 4):
        running = []
        if 0 <= slot - 1 < chips:
            i = slot - 1
            running.append(products(i, kept[i % 3], golds_ref[i % 4]))
        if 0 <= slot - 3 < chips:
            i = slot - 3
            running.append(average(i, kept[i % 3], golds_ref[i % 4]))
        if slot < chips:
            running.append(stage(slot, golds_ref[slot % 4]))
        for dies in groups:
            if slot == dies[-1] + 4:
                running.append(finish_dies(dies))
        while running:
            running = [work for work in running if next(work, running) is not running]

    energy = place([jnp.concatenate(values, 0) for values in refined]) * (1.0 / C)
    sums = zero8
    for i in range(chips):
        found = energy[i * ROWS : (i + 1) * ROWS]
        out_ref[2 * i + core] = found
        mask = own_ref[i, :, half // 2 * LANES :].astype(F32)[:ROWS]
        mask = jnp.where(lane8 < w, mask, 0.0)
        total = jnp.sum(jnp.sum(found * mask, axis=0, keepdims=True), axis=1, keepdims=True)
        count = jnp.sum(jnp.sum(mask, axis=0, keepdims=True), axis=1, keepdims=True)
        both = jnp.where(lane8 == w, total, 0.0) + jnp.where(lane8 == w + 1, count, 0.0)
        sums = sums + jnp.where(sub8 == zones[0][i], both, 0.0)
    for i in range(chips):
        for which in range(2):
            mine = jnp.sum(jnp.where(sub8 == zones[which][i], sums, 0.0), axis=0, keepdims=True)
            mine = jnp.broadcast_to(mine, (ROWS, LANES))
            if which:
                out_ref[2 * i + 1 - core] = mine
            else:
                out_ref[2 * i + core] = out_ref[2 * i + core] + mine


def score_kernel(chips, w, back_ref, out_ref):
    lane = iota((ROWS, LANES), 1)
    total = back_ref[0]
    for d in range(1, 2 * chips):
        total = total + back_ref[d]
    zone_mean = total[:, w : w + 1] / jnp.maximum(total[:, w + 1 : w + 2], 1.0)
    energy = jnp.zeros((ROWS, LANES), F32)
    for p in range(chips):
        strip = back_ref[2 * p] + back_ref[2 * p + 1]
        strip = pltpu.roll(strip, p * w, 1) if p else strip
        energy = jnp.where((lane >= p * w) & (lane < (p + 1) * w), strip, energy)
    out_ref[0] = energy / (zone_mean + 0.01)


def body(n, features, zone_ids, golden_owner, defect_mask, kernels):
    chips = n // 2
    w = defect_mask.shape[2] // chips
    cols = w + 2 * HALO
    half = cols // 2
    raw = w + 4 + 2 * REACH
    length = half * C + LANES
    smem = pl.BlockSpec(memory_space=pltpu.SMEM)
    vmem = pl.BlockSpec(memory_space=pltpu.VMEM)
    params = pltpu.CompilerParams(vmem_limit_bytes=24 * 2**20)

    first = pl.pallas_call(
        first_kernel,
        out_shape=jax.ShapeDtypeStruct((ROWS, LANES), F32),
        out_specs=vmem,
        compiler_params=pltpu.CompilerParams(vmem_limit_bytes=2**20),
        cost_estimate=pl.CostEstimate(flops=10**9, bytes_accessed=10**6, transcendentals=0),
    )()
    packed = pl.pallas_call(
        functools.partial(pack_kernel, chips, w),
        out_shape=jax.ShapeDtypeStruct((chips, 2 * ROWS, length), BF16),
        in_specs=[smem] + [vmem] * 3,
        out_specs=vmem,
        compiler_params=params,
    )(zone_ids, first, features, defect_mask)
    groups = [[2 * p + c for p in range(chips)] for c in range(2)]
    own = lax.all_to_all(packed, "col", 0, 0, axis_index_groups=groups, tiled=True)
    other = lax.ppermute(own, "col", [(d, d ^ 1) for d in range(n)])
    tests = pl.pallas_call(
        functools.partial(test_kernel, chips, w),
        out_shape=[
            jax.ShapeDtypeStruct((chips, raw * ROWS, 4 * LANES), BF16),
            jax.ShapeDtypeStruct((chips, (w + 4) * ROWS, LANES), F32),
        ],
        in_specs=[vmem],
        out_specs=[vmem] * 2,
        scratch_shapes=[
            pltpu.VMEM((chips * (raw // 2) * ROWS, 2 * LANES), F32),
        ]
        + [pltpu.VMEM((raw * SLOT + ROWS, LANES), F32)] * 6
        + [pltpu.VMEM(((w + 4) * SLOT + ROWS, LANES), F32)] * 2,
        compiler_params=params,
        cost_estimate=pl.CostEstimate(flops=10**9, bytes_accessed=10**6, transcendentals=0),
    )(own)
    weights = pl.pallas_call(
        weight_kernel,
        out_shape=jax.ShapeDtypeStruct((2, 12 * C, LANES), BF16),
        in_specs=[vmem],
        out_specs=vmem,
        compiler_params=params,
        cost_estimate=pl.CostEstimate(flops=10**8, bytes_accessed=10**6, transcendentals=0),
    )(jnp.swapaxes(kernels, 1, 2))
    me = lax.axis_index("col").astype(jnp.int32).reshape(1)
    chunks = -(-half // 8)
    reach = [min(raw // 2, 8 * v + 8) - max(0, 8 * v - SHIFT) for v in range(chunks)]
    kept = [
        pltpu.VMEM((2 * reach[v] * ROWS, (2 if half - 8 * v > 4 else 1) * LANES), F32) for v in range(chunks)
    ] + [pltpu.VMEM(((w // 4 + 5) * ROWS, 2 * LANES), F32)]
    rows = half * SLOT + -(-half // 8) * LANES
    partial = pl.pallas_call(
        functools.partial(main_kernel, chips, w),
        out_shape=jax.ShapeDtypeStruct((n, ROWS, LANES), F32),
        in_specs=[smem, smem] + [vmem] * 5,
        out_specs=vmem,
        scratch_shapes=[
            pltpu.VMEM((chips, (w // 2 + 2) * SLOT + ROWS, LANES), F32),
            pltpu.VMEM((chips, (w // 2 + 1) * SLOT + ROWS, LANES), F32),
        ]
        + [pltpu.VMEM((cols * SLOT, LANES), F32)] * 4
        + [pltpu.VMEM((rows, 4 * LANES), BF16)] * 4
        + kept * 3,
        compiler_params=params,
    )(me, golden_owner, own, other, *tests, weights)
    back = lax.all_to_all(partial, "col", 0, 0, tiled=True)
    return pl.pallas_call(
        functools.partial(score_kernel, chips, w),
        out_shape=jax.ShapeDtypeStruct(defect_mask.shape, F32),
        in_specs=[vmem],
        out_specs=vmem,
        compiler_params=params,
    )(back)


def solution(mesh):
    split = P(("groups", "col"), None, None)
    return jax.shard_map(
        functools.partial(body, mesh.shape["col"]),
        mesh=mesh,
        in_specs=(split, P(("groups", "col")), P("groups"), split, P()),
        out_specs=split,
        check_vma=False,
    )
```

```python
import functools

import jax
import jax.numpy as jnp
from jax import lax
from jax.experimental import pallas as pl
from jax.experimental.pallas import tpu as pltpu
from jax.sharding import PartitionSpec as P

C = 64
SHIFT = 6
BOX = 5
Z = 8
SIDE = 2 * SHIFT + 1
REACH = BOX // 2
HALO = SHIFT + REACH + 2
ROWS = 8
SLOT = 16
TOP = (SLOT - ROWS) // 2
LANES = 128
FACTOR = 32.0 * 1.4426950408889634
F32 = jnp.float32
BF16 = jnp.bfloat16


def iota(shape, dim):
    return lax.broadcasted_iota(jnp.int32, shape, dim)


def first_kernel(out_ref):
    out_ref[...] = jnp.zeros((ROWS, LANES), F32)


def pack_kernel(chips, w, zone_ref, first_ref, feat_ref, mask_ref, out_ref):
    cols = w + 2 * HALO
    width = mask_ref.shape[2]
    mask = mask_ref[0].astype(F32)
    zone = first_ref[...] + zone_ref[0].astype(F32)
    lane = iota((ROWS, LANES), 1)
    for p in range(chips):
        for t in range(cols // 2):
            col = p * w - HALO + 2 * t
            at = slice(t * LANES, (t + 1) * LANES)
            if 0 <= col < width:
                out_ref[p, :, at] = feat_ref[0, :, col * C : (col + 2) * C]
            else:
                out_ref[p, :, at] = jnp.zeros((ROWS, LANES), BF16)
        here = pltpu.roll(mask, (width - p * w) % width, 1) if p else mask
        out_ref[p, :, cols * C :] = jnp.where(lane < w, here, zone).astype(BF16)


def pair_of(ref, i, t):
    return ref[i, :, t * LANES : (t + 1) * LANES].astype(F32)


def split_square(values):
    square = values * values
    high = square.astype(BF16).astype(F32)
    return high, square - high


def place(values):
    row, col = iota((LANES, LANES), 0), iota((LANES, LANES), 1)
    highs, lows = zip(*(split_square(value) for value in values))
    squares = [jnp.concatenate([part.astype(BF16) for part in parts], 1) for parts in (highs, lows)]
    picks = [(col == 2 * q + row // C).astype(BF16) for q in range(len(values))]
    sums = jnp.dot(jnp.concatenate(squares, 0), jnp.concatenate(picks, 0), preferred_element_type=F32)
    rows = sums.shape[0] // 2
    return sums[:rows] + sums[rows:]


def test_kernel(chips, w, own_ref, test_ref, box_ref, wide_ref, *scratch):
    raw = w + 4 + 2 * REACH
    before = HALO - REACH - 2
    zero8 = jnp.zeros((ROWS, LANES), F32)
    lo, hi = slice(0, C), slice(C, LANES)

    for ref in scratch:
        for i in range(0, ref.shape[0], ROWS):
            ref[i : i + ROWS, :] = zero8
    pairs = []
    for t in range(before // 2, (before + raw) // 2):
        pairs.append([pair_of(own_ref, i, t) for i in range(chips)])
    parts = [split_square(jnp.concatenate([tiles[i] for tiles in pairs], 0)) for i in range(chips)]
    squares = [jnp.concatenate([part[k].astype(BF16) for part in parts], 0) for k in range(2)]
    both = (iota((2 * LANES, 2 * LANES), 0) % LANES // C == iota((2 * LANES, 2 * LANES), 1) // LANES).astype(BF16)
    wide_ref[...] = jnp.dot(jnp.concatenate(squares, 1), both, preferred_element_type=F32)
    scale = 1.0 / FACTOR**2
    for i in range(chips):
        energy = []
        for r in range(raw):
            row = (i * (raw // 2) + r // 2) * ROWS
            energy.append(wide_ref[row : row + ROWS, r % 2 * LANES : (r % 2 + 1) * LANES])
        twos = [x + y for x, y in zip(energy, energy[1:])]
        ref = scratch[6 + i % 2]
        for l in range(w + 4):
            ref[l * SLOT + ROWS : (l + 1) * SLOT, :] = (twos[l] + twos[l + 2] + energy[l + 4]) * scale
        for l in range(w + 4):
            base = l * SLOT + ROWS
            rows = [ref[base + dy : base + dy + ROWS, :] for dy in range(-2, 3)]
            box_ref[i, l * ROWS : (l + 1) * ROWS, :] = sum(rows[1:], rows[0])

    for i in range(chips):
        refs = scratch[3 * (i % 2) : 3 * (i % 2) + 3]
        for q in range(raw // 2):
            here = pairs[q][i]
            turned = pltpu.roll(here, C, 1)
            for odd, (left, right) in enumerate(((here, turned), (turned, here))):
                top = (2 * q + odd) * SLOT + ROWS
                refs[0][top + 2 : top + 2 + ROWS, lo] = left[:, lo]
                refs[0][top + 1 : top + 1 + ROWS, hi] = right[:, hi]
                refs[1][top : top + ROWS, lo] = left[:, lo]
                refs[2][top - 1 : top - 1 + ROWS, lo] = left[:, lo]
                refs[2][top - 2 : top - 2 + ROWS, hi] = right[:, hi]
        for r in range(0, raw, 2):
            at = slice(r * ROWS, (r + 2) * ROWS)
            for t, ref in enumerate(refs):
                two = [ref[q * SLOT + ROWS : (q + 1) * SLOT, :] for q in (r, r + 1)]
                test_ref[i, at, t * LANES : (t + 1) * LANES] = jnp.concatenate(two, 0).astype(BF16)
            test_ref[i, at, 3 * LANES :] = jnp.zeros((2 * ROWS, LANES), BF16)


def weight_kernel(kern_ref, weight_ref):
    twice = (iota((C, LANES), 1) % C == iota((C, LANES), 0)).astype(BF16)
    low = iota((C, LANES), 1) < C
    for conv in range(2):
        doubled = lax.dot_general(kern_ref[conv], twice, (((0,), (0,)), ((), ())), preferred_element_type=F32)
        for dy in range(3):
            for at in range(4):
                taps = [
                    doubled[(3 * dy + dx) * C : (3 * dy + dx + 1) * C] if 0 <= dx < 3 else jnp.zeros((C, LANES), F32)
                    for dx in (at, at - 1)
                ]
                row = (4 * dy + at) * C
                weight_ref[conv, row : row + C, :] = jnp.where(low, taps[0], taps[1]).astype(BF16)


def main_kernel(
    chips, w, me_ref, owner_ref, own_ref, other_ref, test_ref, box_ref, weight_ref, out_ref,
    res_ref, hid_ref, g0_ref, g1_ref, g2_ref, gsq_ref, *scratch
):
    cols = w + 2 * HALO
    half = cols // 2
    raw = w + 4 + 2 * REACH
    outs = w + 4
    odds = half * SLOT
    chunks = -(-half // 8)
    lanes_g = chunks * LANES
    golds_ref = scratch[:4]
    kept = [scratch[4 + k * (chunks + 1) : 4 + (k + 1) * (chunks + 1)] for k in range(3)]
    me = me_ref[0]
    chip = me // 2
    core = me % 2
    not_first = jnp.where(chip == 0, 0.0, 1.0).astype(F32)
    not_last = jnp.where(chip == chips - 1, 0.0, 1.0).astype(F32)

    lane8 = iota((ROWS, LANES), 1)
    sub8 = iota((ROWS, LANES), 0)
    low8 = lane8 < C
    zero8 = jnp.zeros((ROWS, LANES), F32)
    lo = slice(0, C)
    hi = slice(C, LANES)

    zones = [
        [pair_of(ref, i, cols // 2)[0, w].astype(jnp.int32) for i in range(chips)] for ref in (own_ref, other_ref)
    ]
    golds = [owner_ref[zone] for zone in zones[0]]

    for ref in (g0_ref, g1_ref, g2_ref, gsq_ref):
        for i in range(0, ref.shape[0], ROWS):
            ref[i : i + ROWS, :] = jnp.where(low8, 0.0, 1.0) if ref is g1_ref else zero8
    if half % 8 > 4:
        for ref in golds_ref:
            ref[cols * SLOT :, :] = jnp.zeros((ref.shape[0] - cols * SLOT, 4 * LANES), BF16)
    summing = (iota((SLOT, 4 * LANES), 1) >= 3 * LANES).astype(BF16)

    valid = []
    for k in range(4):
        a = lane8 % SLOT - TOP - sub8
        both = []
        for parity in range(2):
            b = lane8 // SLOT * 2 + parity - k
            both.append((b >= 0) & (b < SIDE) & (jnp.abs(a) <= SHIFT))
        valid.append(both)
    outside = jnp.maximum(SHIFT - TOP - sub8, 0) + jnp.maximum(sub8 + SHIFT - (SLOT - TOP - 1), 0)
    outside = (outside * SIDE).astype(F32)

    def stage(i, gold_ref):
        owner = golds[i]
        mine = owner % 2 == core
        for t in range(cols // 2):
            here = jnp.where(mine, pair_of(own_ref, owner // 2, t), pair_of(other_ref, owner // 2, t))
            turned = pltpu.roll(here, C, 1)
            for odd, (left, right) in enumerate(((here, turned), (turned, here))):
                top = odd * odds + t * SLOT + TOP
                g0_ref[top + 2 : top + 2 + ROWS, lo] = left[:, lo]
                g0_ref[top + 1 : top + 1 + ROWS, hi] = right[:, hi]
                g1_ref[top : top + ROWS, lo] = left[:, lo]
                g2_ref[top - 1 : top - 1 + ROWS, lo] = left[:, lo]
                g2_ref[top - 2 : top - 2 + ROWS, hi] = right[:, hi]
                high, low = split_square(jnp.where(low8, left, right))
                gsq_ref[top : top + ROWS, :] = jnp.where(low8, high, low)
            yield
        for parity in range(2):
            for g in range(half):
                at = slice(parity * odds + g * SLOT, parity * odds + (g + 1) * SLOT)
                for t, ref in enumerate((g0_ref, g1_ref, g2_ref, gsq_ref)):
                    gold_ref[at, t * LANES : (t + 1) * LANES] = ref[at, :].astype(BF16)
                if g % 6 == 5:
                    yield

    def right(value, slots):
        return pltpu.roll(value, slots * SLOT, 1) if slots else value

    def windows(gold_ref, tile, at):
        rows = [slice(p * odds + tile * SLOT, p * odds + (tile + 8) * SLOT) for p in range(2)]
        return jnp.concatenate([gold_ref[rows[0], at], gold_ref[rows[1], at]], 0)

    def first_pair(v):
        return max(0, 8 * v - SHIFT)

    def products(i, kept, gold_ref):
        energies = ([], [])
        for v in range(chunks):
            first, last = first_pair(v), min(raw // 2 - 1, 8 * v + 7)
            tiles = min(8, half - 8 * v)
            rows = [slice(p * odds + 8 * v * SLOT, p * odds + (8 * v + (tiles if tiles <= 4 else 8)) * SLOT) for p in range(2)]
            parts = [gold_ref[rows[0], :], gold_ref[rows[1], :]]
            if tiles < 4:
                parts.append(gold_ref[: (8 - 2 * tiles) * SLOT, :])
            block = lax.dot_general(
                jnp.concatenate([summing, test_ref[i, 2 * first * ROWS : 2 * (last + 1) * ROWS, :]], 0),
                jnp.concatenate(parts, 0),
                (((1,), (1,)), ((), ())),
                preferred_element_type=F32,
            )
            for p in range(2):
                at = slice(p * LANES, (p + 1) * LANES) if tiles > 4 else slice(0, LANES)
                start = 0 if tiles > 4 else p * tiles * SLOT
                here = block[:ROWS, at]
                energies[p].append(pltpu.roll(here, LANES - start, 1) if start else here)
            kept[v][...] = block[SLOT:]
            yield

        by_parity = []
        for parity in range(2):
            parts = []
            for here in energies[parity]:
                down = here
                for dy in (-2, -1, 1, 2):
                    inside = (sub8 + dy >= 0) & (sub8 + dy < ROWS)
                    down = down + jnp.where(inside, pltpu.roll(here, (-dy) % LANES, 1), 0.0)
                parts.append(down)
            by_parity.append(jnp.concatenate(parts, 1))
        even, odd = by_parity
        even1, even2 = (pltpu.roll(even, lanes_g - d * SLOT, 1) for d in (1, 2))
        odd1, odd2 = (pltpu.roll(odd, lanes_g - d * SLOT, 1) for d in (1, 2))
        def window(values, m):
            v, offset = divmod(2 * m * SLOT, LANES)
            first = values[:, v * LANES : (v + 1) * LANES]
            if not offset:
                return first
            second = values[:, (v + 1) * LANES : (v + 2) * LANES]
            return pltpu.roll(jnp.where(lane8 >= offset, first, second), LANES - offset, 1)

        for p, terms in enumerate(((even, odd, even1, odd1, even2), (odd, even1, odd1, even2, odd2))):
            a, b, c, d, e = terms
            rows = [(m, a + b + c + d + e) for m in range(outs // 4)]
            rows.append((0, c + d + e + not_first * (a + b)))
            rows.append((0, b + c + d + e + not_first * a))
            rows.append((w // 4, a + b + c + d + not_last * e))
            rows.append((w // 4, a + b + c + not_last * (d + e)))
            for row, (m, values) in enumerate(rows):
                kept[chunks][row * ROWS : (row + 1) * ROWS, p * LANES : (p + 1) * LANES] = window(values, m)
            yield

    def average(i, kept, gold_ref):
        special = {l: outs // 4 + k for k, l in enumerate((2, 3, w, w + 1))}

        def piece(r, parity, v):
            row = (r - 2 * first_pair(v)) * ROWS
            tiles = half - 8 * v
            if tiles > 4:
                return kept[v][row : row + ROWS, parity * LANES : (parity + 1) * LANES], 0
            return kept[v][row : row + ROWS, :], parity * tiles * SLOT

        def shear(r, parity, more):
            v, slots = divmod(r // 2 + more, 8)
            value, start = piece(r, parity, v)
            if slots + SHIFT - more >= 8:
                value2, start2 = piece(r, parity, v + 1)
                if start2:
                    value2 = pltpu.roll(value2, LANES - start2, 1)
                value = jnp.where(lane8 >= slots * SLOT, value, value2)
            turn = start + slots * SLOT
            return pltpu.roll(value, LANES - turn, 1) if turn else value

        def finish(m, weight):
            values = windows(gold_ref, 2 * m + 1, slice(LANES, 2 * LANES))
            total = jnp.dot(weight, values, preferred_element_type=F32)
            for k in (0, 2):
                pair = (4 * m + k) // 2
                even, odd = total[k * ROWS : (k + 1) * ROWS], total[(k + 1) * ROWS : (k + 2) * ROWS]
                numer = jnp.where(low8, even, pltpu.roll(odd, C, 1))
                denom = jnp.where(low8, pltpu.roll(even, C, 1), odd) + outside
                value = pair_of(own_ref, i, HALO // 2 - 1 + pair) - numer / denom
                if pair == 0:
                    value = value * not_first
                if pair == outs // 2 - 1:
                    value = value * not_last
                res_ref[i, pair * SLOT + ROWS : (pair + 1) * SLOT, :] = value.astype(BF16).astype(F32)

        sheared, pairs = [], []

        def extend(count):
            for r in range(len(sheared), count):
                odd = r % 2
                sheared.append((shear(r, odd, 0), shear(r, 1 - odd, odd)))
                if r:
                    pairs.append(tuple(x + y for x, y in zip(sheared[r - 1], sheared[r])))

        for m in range(outs // 4):
            extend(4 * m + 8)
            chosen = []
            for k in range(4):
                l = 4 * m + k
                cross = [pairs[l][b] + pairs[l + 2][b] + sheared[l + 4][b] for b in range(2)]
                cross = [right(cross[k % 2], (k + 1) // 2 if k % 2 else k // 2), right(cross[1 - k % 2], k // 2)]
                mine = box_ref[i, l * ROWS : (l + 1) * ROWS, :]
                row = special.get(l, m) * ROWS
                both = []
                for p in range(2):
                    other = kept[chunks][row : row + ROWS, p * LANES : (p + 1) * LANES]
                    scale = lax.rsqrt(mine * other + 1e-05 / FACTOR**2)
                    both.append(jnp.where(valid[k][p], jnp.exp2(cross[p] * scale), 0.0))
                chosen.append(jnp.concatenate(both, 1))
            weight = jnp.concatenate(chosen, 0).astype(BF16)
            if m:
                finish(m - 1, before)
            before = weight
            yield
        finish(outs // 4 - 1, before)
        yield

    for i in range(chips):
        for x in range(outs // 2 + 1):
            res_ref[i, x * SLOT : x * SLOT + ROWS, :] = zero8
        for x in range(w // 2 + 2):
            hid_ref[i, x * SLOT : x * SLOT + ROWS, :] = zero8
    def convolve(ref, count, weight, dies):
        tiles = []
        for dy in (-1, 0, 1):
            for which in range(2):
                rows = [
                    ref[i, (p + which) * SLOT + ROWS + dy : (p + which + 1) * SLOT + dy, :]
                    for i in dies
                    for p in range(count)
                ]
                tiles.append(jnp.concatenate(rows, 0).astype(BF16))
        full = jnp.dot(jnp.concatenate(tiles, 1), weight, preferred_element_type=F32)
        return [
            (i, [full[(k * count + p) * ROWS : (k * count + p + 1) * ROWS] for p in range(count)])
            for k, i in enumerate(dies)
        ]

    def finish_dies(dies):
        for i, values in convolve(res_ref, outs // 2 - 1, weight_ref[0], dies):
            for p, value in enumerate(values):
                value = jnp.maximum(value, 0.0).astype(BF16).astype(F32)
                if p == 0:
                    value = jnp.where(low8, value * not_first, value)
                if p == w // 2:
                    value = jnp.where(low8, value, value * not_last)
                hid_ref[i, p * SLOT + ROWS : (p + 1) * SLOT, :] = value
        yield
        for i, values in convolve(hid_ref, w // 2, weight_ref[1], dies):
            for p, value in enumerate(values):
                refined[p].append(res_ref[i, (p + 1) * SLOT + ROWS : (p + 2) * SLOT, :] + value)
        yield

    refined = [[] for p in range(w // 2)]
    groups, sizes = [], [3, 3, 2] if chips == 8 else [4] * (chips // 4)
    for size in sizes:
        groups.append(range(sum(map(len, groups)), sum(map(len, groups)) + size))
    for slot in range(chips + 4):
        running = []
        if 0 <= slot - 1 < chips:
            i = slot - 1
            running.append(products(i, kept[i % 3], golds_ref[i % 4]))
        if 0 <= slot - 3 < chips:
            i = slot - 3
            running.append(average(i, kept[i % 3], golds_ref[i % 4]))
        if slot < chips:
            running.append(stage(slot, golds_ref[slot % 4]))
        for dies in groups:
            if slot == dies[-1] + 4:
                running.append(finish_dies(dies))
        while running:
            running = [work for work in running if next(work, running) is not running]

    energy = place([jnp.concatenate(values, 0) for values in refined]) * (1.0 / C)
    sums = zero8
    for i in range(chips):
        found = energy[i * ROWS : (i + 1) * ROWS]
        out_ref[2 * i + core] = found
        mask = jnp.where(lane8 < w, pair_of(own_ref, i, cols // 2), 0.0)
        total = jnp.sum(jnp.sum(found * mask, axis=0, keepdims=True), axis=1, keepdims=True)
        count = jnp.sum(jnp.sum(mask, axis=0, keepdims=True), axis=1, keepdims=True)
        both = jnp.where(lane8 == w, total, 0.0) + jnp.where(lane8 == w + 1, count, 0.0)
        sums = sums + jnp.where(sub8 == zones[0][i], both, 0.0)
    for i in range(chips):
        for which in range(2):
            mine = jnp.sum(jnp.where(sub8 == zones[which][i], sums, 0.0), axis=0, keepdims=True)
            mine = jnp.broadcast_to(mine, (ROWS, LANES))
            if which:
                out_ref[2 * i + 1 - core] = mine
            else:
                out_ref[2 * i + core] = out_ref[2 * i + core] + mine


def score_kernel(chips, w, back_ref, out_ref):
    lane = iota((ROWS, LANES), 1)
    total = back_ref[0]
    for d in range(1, 2 * chips):
        total = total + back_ref[d]
    zone_mean = total[:, w : w + 1] / jnp.maximum(total[:, w + 1 : w + 2], 1.0)
    energy = jnp.zeros((ROWS, LANES), F32)
    for p in range(chips):
        strip = back_ref[2 * p] + back_ref[2 * p + 1]
        strip = pltpu.roll(strip, p * w, 1) if p else strip
        energy = jnp.where((lane >= p * w) & (lane < (p + 1) * w), strip, energy)
    out_ref[0] = energy / (zone_mean + 0.01)


def body(n, features, zone_ids, golden_owner, defect_mask, kernels):
    chips = n // 2
    w = defect_mask.shape[2] // chips
    cols = w + 2 * HALO
    half = cols // 2
    raw = w + 4 + 2 * REACH
    length = cols * C + LANES
    smem = pl.BlockSpec(memory_space=pltpu.SMEM)
    vmem = pl.BlockSpec(memory_space=pltpu.VMEM)
    params = pltpu.CompilerParams(vmem_limit_bytes=24 * 2**20)

    first = pl.pallas_call(
        first_kernel,
        out_shape=jax.ShapeDtypeStruct((ROWS, LANES), F32),
        out_specs=vmem,
        compiler_params=pltpu.CompilerParams(vmem_limit_bytes=2**20),
        cost_estimate=pl.CostEstimate(flops=10**9, bytes_accessed=10**6, transcendentals=0),
    )()
    packed = pl.pallas_call(
        functools.partial(pack_kernel, chips, w),
        out_shape=jax.ShapeDtypeStruct((chips, ROWS, length), BF16),
        in_specs=[smem] + [vmem] * 3,
        out_specs=vmem,
        compiler_params=params,
    )(zone_ids, first, features, defect_mask)
    groups = [[2 * p + c for p in range(chips)] for c in range(2)]
    own = lax.all_to_all(packed, "col", 0, 0, axis_index_groups=groups, tiled=True)
    other = lax.ppermute(own, "col", [(d, d ^ 1) for d in range(n)])
    tests = pl.pallas_call(
        functools.partial(test_kernel, chips, w),
        out_shape=[
            jax.ShapeDtypeStruct((chips, raw * ROWS, 4 * LANES), BF16),
            jax.ShapeDtypeStruct((chips, (w + 4) * ROWS, LANES), F32),
        ],
        in_specs=[vmem],
        out_specs=[vmem] * 2,
        scratch_shapes=[
            pltpu.VMEM((chips * (raw // 2) * ROWS, 2 * LANES), F32),
        ]
        + [pltpu.VMEM((raw * SLOT + ROWS, LANES), F32)] * 6
        + [pltpu.VMEM(((w + 4) * SLOT + ROWS, LANES), F32)] * 2,
        compiler_params=params,
        cost_estimate=pl.CostEstimate(flops=10**9, bytes_accessed=10**6, transcendentals=0),
    )(own)
    weights = pl.pallas_call(
        weight_kernel,
        out_shape=jax.ShapeDtypeStruct((2, 12 * C, LANES), BF16),
        in_specs=[vmem],
        out_specs=vmem,
        compiler_params=params,
        cost_estimate=pl.CostEstimate(flops=10**8, bytes_accessed=10**6, transcendentals=0),
    )(jnp.swapaxes(kernels, 1, 2))
    me = lax.axis_index("col").astype(jnp.int32).reshape(1)
    chunks = -(-half // 8)
    reach = [min(raw // 2, 8 * v + 8) - max(0, 8 * v - SHIFT) for v in range(chunks)]
    kept = [
        pltpu.VMEM((2 * reach[v] * ROWS, (2 if half - 8 * v > 4 else 1) * LANES), F32) for v in range(chunks)
    ] + [pltpu.VMEM(((w // 4 + 5) * ROWS, 2 * LANES), F32)]
    rows = half * SLOT + -(-half // 8) * LANES
    partial = pl.pallas_call(
        functools.partial(main_kernel, chips, w),
        out_shape=jax.ShapeDtypeStruct((n, ROWS, LANES), F32),
        in_specs=[smem, smem] + [vmem] * 5,
        out_specs=vmem,
        scratch_shapes=[
            pltpu.VMEM((chips, (w // 2 + 2) * SLOT + ROWS, LANES), F32),
            pltpu.VMEM((chips, (w // 2 + 1) * SLOT + ROWS, LANES), F32),
        ]
        + [pltpu.VMEM((cols * SLOT, LANES), F32)] * 4
        + [pltpu.VMEM((rows, 4 * LANES), BF16)] * 4
        + kept * 3,
        compiler_params=params,
    )(me, golden_owner, own, other, *tests, weights)
    back = lax.all_to_all(partial, "col", 0, 0, tiled=True)
    return pl.pallas_call(
        functools.partial(score_kernel, chips, w),
        out_shape=jax.ShapeDtypeStruct(defect_mask.shape, F32),
        in_specs=[vmem],
        out_specs=vmem,
        compiler_params=params,
    )(back)


def solution(mesh):
    split = P(("groups", "col"), None, None)
    return jax.shard_map(
        functools.partial(body, mesh.shape["col"]),
        mesh=mesh,
        in_specs=(split, P(("groups", "col")), P("groups"), split, P()),
        out_specs=split,
        check_vma=False,
    )
```

```python
import functools

import jax
import jax.numpy as jnp
from jax import lax
from jax.experimental import pallas as pl
from jax.experimental.pallas import tpu as pltpu
from jax.sharding import PartitionSpec as P

C = 64
SHIFT = 6
BOX = 5
Z = 8
SIDE = 2 * SHIFT + 1
REACH = BOX // 2
HALO = SHIFT + REACH + 2
ROWS = 8
SLOT = 16
TOP = (SLOT - ROWS) // 2
LANES = 128
FACTOR = 32.0 * 1.4426950408889634
F32 = jnp.float32
BF16 = jnp.bfloat16


def iota(shape, dim):
    return lax.broadcasted_iota(jnp.int32, shape, dim)


def first_kernel(out_ref):
    out_ref[...] = jnp.zeros((ROWS, LANES), F32)


def pack_kernel(chips, w, zone_ref, first_ref, feat_ref, mask_ref, out_ref):
    cols = w + 2 * HALO
    width = mask_ref.shape[2]
    mask = mask_ref[0].astype(F32)
    zone = first_ref[...] + zone_ref[0].astype(F32)
    lane = iota((ROWS, LANES), 1)
    for p in range(chips):
        for t in range(cols // 2):
            col = p * w - HALO + 2 * t
            at = slice(t * LANES, (t + 1) * LANES)
            if 0 <= col < width:
                out_ref[p, :, at] = feat_ref[0, :, col * C : (col + 2) * C]
            else:
                out_ref[p, :, at] = jnp.zeros((ROWS, LANES), BF16)
        here = pltpu.roll(mask, (width - p * w) % width, 1) if p else mask
        out_ref[p, :, cols * C :] = jnp.where(lane < w, here, zone).astype(BF16)


def pair_of(ref, i, t):
    return ref[i, :, t * LANES : (t + 1) * LANES].astype(F32)


def split_square(values):
    square = values * values
    high = square.astype(BF16).astype(F32)
    return high, square - high


def place(values):
    row, col = iota((LANES, LANES), 0), iota((LANES, LANES), 1)
    highs, lows = zip(*(split_square(value) for value in values))
    squares = [jnp.concatenate([part.astype(BF16) for part in parts], 1) for parts in (highs, lows)]
    picks = [(col == 2 * q + row // C).astype(BF16) for q in range(len(values))]
    sums = jnp.dot(jnp.concatenate(squares, 0), jnp.concatenate(picks, 0), preferred_element_type=F32)
    rows = sums.shape[0] // 2
    return sums[:rows] + sums[rows:]


def test_kernel(chips, w, own_ref, test_ref, box_ref, wide_ref, *scratch):
    raw = w + 4 + 2 * REACH
    before = HALO - REACH - 2
    zero8 = jnp.zeros((ROWS, LANES), F32)
    lo, hi = slice(0, C), slice(C, LANES)

    for ref in scratch:
        for i in range(0, ref.shape[0], ROWS):
            ref[i : i + ROWS, :] = zero8
    pairs = []
    for t in range(before // 2, (before + raw) // 2):
        pairs.append([pair_of(own_ref, i, t) for i in range(chips)])
    parts = [split_square(jnp.concatenate([tiles[i] for tiles in pairs], 0)) for i in range(chips)]
    squares = [jnp.concatenate([part[k].astype(BF16) for part in parts], 0) for k in range(2)]
    both = (iota((2 * LANES, 2 * LANES), 0) % LANES // C == iota((2 * LANES, 2 * LANES), 1) // LANES).astype(BF16)
    wide_ref[...] = jnp.dot(jnp.concatenate(squares, 1), both, preferred_element_type=F32)
    scale = 1.0 / FACTOR**2
    for i in range(chips):
        energy = []
        for r in range(raw):
            row = (i * (raw // 2) + r // 2) * ROWS
            energy.append(wide_ref[row : row + ROWS, r % 2 * LANES : (r % 2 + 1) * LANES])
        twos = [x + y for x, y in zip(energy, energy[1:])]
        ref = scratch[6 + i % 2]
        for l in range(w + 4):
            ref[l * SLOT + ROWS : (l + 1) * SLOT, :] = (twos[l] + twos[l + 2] + energy[l + 4]) * scale
        for l in range(w + 4):
            base = l * SLOT + ROWS
            rows = [ref[base + dy : base + dy + ROWS, :] for dy in range(-2, 3)]
            box_ref[i, l * ROWS : (l + 1) * ROWS, :] = sum(rows[1:], rows[0])

    for i in range(chips):
        refs = scratch[3 * (i % 2) : 3 * (i % 2) + 3]
        for q in range(raw // 2):
            here = pairs[q][i]
            turned = pltpu.roll(here, C, 1)
            for odd, (left, right) in enumerate(((here, turned), (turned, here))):
                top = (2 * q + odd) * SLOT + ROWS
                refs[0][top + 2 : top + 2 + ROWS, lo] = left[:, lo]
                refs[0][top + 1 : top + 1 + ROWS, hi] = right[:, hi]
                refs[1][top : top + ROWS, lo] = left[:, lo]
                refs[2][top - 1 : top - 1 + ROWS, lo] = left[:, lo]
                refs[2][top - 2 : top - 2 + ROWS, hi] = right[:, hi]
        for r in range(0, raw, 2):
            at = slice(r * ROWS, (r + 2) * ROWS)
            for t, ref in enumerate(refs):
                two = [ref[q * SLOT + ROWS : (q + 1) * SLOT, :] for q in (r, r + 1)]
                test_ref[i, at, t * LANES : (t + 1) * LANES] = jnp.concatenate(two, 0).astype(BF16)
            test_ref[i, at, 3 * LANES :] = jnp.zeros((2 * ROWS, LANES), BF16)


def weight_kernel(kern_ref, weight_ref):
    twice = (iota((C, LANES), 1) % C == iota((C, LANES), 0)).astype(BF16)
    low = iota((C, LANES), 1) < C
    for conv in range(2):
        doubled = lax.dot_general(kern_ref[conv], twice, (((0,), (0,)), ((), ())), preferred_element_type=F32)
        for dy in range(3):
            for at in range(4):
                taps = [
                    doubled[(3 * dy + dx) * C : (3 * dy + dx + 1) * C] if 0 <= dx < 3 else jnp.zeros((C, LANES), F32)
                    for dx in (at, at - 1)
                ]
                row = (4 * dy + at) * C
                weight_ref[conv, row : row + C, :] = jnp.where(low, taps[0], taps[1]).astype(BF16)


def main_kernel(
    chips, w, me_ref, owner_ref, own_ref, other_ref, test_ref, box_ref, weight_ref, out_ref,
    res_ref, hid_ref, g0_ref, g1_ref, g2_ref, gsq_ref, *scratch
):
    cols = w + 2 * HALO
    half = cols // 2
    raw = w + 4 + 2 * REACH
    outs = w + 4
    odds = half * SLOT
    chunks = -(-half // 8)
    lanes_g = chunks * LANES
    golds_ref = scratch[:5]
    kept = [scratch[5 + k * (chunks + 1) : 5 + (k + 1) * (chunks + 1)] for k in range(4)]
    me = me_ref[0]
    chip = me // 2
    core = me % 2
    not_first = jnp.where(chip == 0, 0.0, 1.0).astype(F32)
    not_last = jnp.where(chip == chips - 1, 0.0, 1.0).astype(F32)

    lane8 = iota((ROWS, LANES), 1)
    sub8 = iota((ROWS, LANES), 0)
    low8 = lane8 < C
    zero8 = jnp.zeros((ROWS, LANES), F32)
    lo = slice(0, C)
    hi = slice(C, LANES)

    zones = [
        [pair_of(ref, i, cols // 2)[0, w].astype(jnp.int32) for i in range(chips)] for ref in (own_ref, other_ref)
    ]
    golds = [owner_ref[zone] for zone in zones[0]]

    for ref in (g0_ref, g1_ref, g2_ref, gsq_ref):
        for i in range(0, ref.shape[0], ROWS):
            ref[i : i + ROWS, :] = jnp.where(low8, 0.0, 1.0) if ref is g1_ref else zero8
    if half % 8 > 4:
        for ref in golds_ref:
            ref[cols * SLOT :, :] = jnp.zeros((ref.shape[0] - cols * SLOT, 4 * LANES), BF16)
    summing = (iota((SLOT, 4 * LANES), 1) >= 3 * LANES).astype(BF16)

    valid = []
    for k in range(4):
        a = lane8 % SLOT - TOP - sub8
        both = []
        for parity in range(2):
            b = lane8 // SLOT * 2 + parity - k
            both.append((b >= 0) & (b < SIDE) & (jnp.abs(a) <= SHIFT))
        valid.append(both)
    outside = jnp.maximum(SHIFT - TOP - sub8, 0) + jnp.maximum(sub8 + SHIFT - (SLOT - TOP - 1), 0)
    outside = (outside * SIDE).astype(F32)

    def stage(i, gold_ref):
        owner = golds[i]
        mine = owner % 2 == core
        for t in range(cols // 2):
            here = jnp.where(mine, pair_of(own_ref, owner // 2, t), pair_of(other_ref, owner // 2, t))
            turned = pltpu.roll(here, C, 1)
            for odd, (left, right) in enumerate(((here, turned), (turned, here))):
                top = odd * odds + t * SLOT + TOP
                g0_ref[top + 2 : top + 2 + ROWS, lo] = left[:, lo]
                g0_ref[top + 1 : top + 1 + ROWS, hi] = right[:, hi]
                g1_ref[top : top + ROWS, lo] = left[:, lo]
                g2_ref[top - 1 : top - 1 + ROWS, lo] = left[:, lo]
                g2_ref[top - 2 : top - 2 + ROWS, hi] = right[:, hi]
                high, low = split_square(jnp.where(low8, left, right))
                gsq_ref[top : top + ROWS, :] = jnp.where(low8, high, low)
            yield
        for parity in range(2):
            for g in range(half):
                at = slice(parity * odds + g * SLOT, parity * odds + (g + 1) * SLOT)
                for t, ref in enumerate((g0_ref, g1_ref, g2_ref, gsq_ref)):
                    gold_ref[at, t * LANES : (t + 1) * LANES] = ref[at, :].astype(BF16)
                if g % 6 == 5:
                    yield

    def right(value, slots):
        return pltpu.roll(value, slots * SLOT, 1) if slots else value

    def windows(gold_ref, tile, at):
        rows = [slice(p * odds + tile * SLOT, p * odds + (tile + 8) * SLOT) for p in range(2)]
        return jnp.concatenate([gold_ref[rows[0], at], gold_ref[rows[1], at]], 0)

    def first_pair(v):
        return max(0, 8 * v - SHIFT)

    def products(i, kept, gold_ref):
        energies = ([], [])
        for v in range(chunks):
            first, last = first_pair(v), min(raw // 2 - 1, 8 * v + 7)
            tiles = min(8, half - 8 * v)
            rows = [slice(p * odds + 8 * v * SLOT, p * odds + (8 * v + (tiles if tiles <= 4 else 8)) * SLOT) for p in range(2)]
            parts = [gold_ref[rows[0], :], gold_ref[rows[1], :]]
            if tiles < 4:
                parts.append(gold_ref[: (8 - 2 * tiles) * SLOT, :])
            block = lax.dot_general(
                jnp.concatenate([summing, test_ref[i, 2 * first * ROWS : 2 * (last + 1) * ROWS, :]], 0),
                jnp.concatenate(parts, 0),
                (((1,), (1,)), ((), ())),
                preferred_element_type=F32,
            )
            for p in range(2):
                at = slice(p * LANES, (p + 1) * LANES) if tiles > 4 else slice(0, LANES)
                start = 0 if tiles > 4 else p * tiles * SLOT
                here = block[:ROWS, at]
                energies[p].append(pltpu.roll(here, LANES - start, 1) if start else here)
            kept[v][...] = block[SLOT:]
            yield

        by_parity = []
        for parity in range(2):
            parts = []
            for here in energies[parity]:
                down = here
                for dy in (-2, -1, 1, 2):
                    inside = (sub8 + dy >= 0) & (sub8 + dy < ROWS)
                    down = down + jnp.where(inside, pltpu.roll(here, (-dy) % LANES, 1), 0.0)
                parts.append(down)
            by_parity.append(jnp.concatenate(parts, 1))
        even, odd = by_parity
        even1, even2 = (pltpu.roll(even, lanes_g - d * SLOT, 1) for d in (1, 2))
        odd1, odd2 = (pltpu.roll(odd, lanes_g - d * SLOT, 1) for d in (1, 2))
        def window(values, m):
            v, offset = divmod(2 * m * SLOT, LANES)
            first = values[:, v * LANES : (v + 1) * LANES]
            if not offset:
                return first
            second = values[:, (v + 1) * LANES : (v + 2) * LANES]
            return pltpu.roll(jnp.where(lane8 >= offset, first, second), LANES - offset, 1)

        for p, terms in enumerate(((even, odd, even1, odd1, even2), (odd, even1, odd1, even2, odd2))):
            a, b, c, d, e = terms
            rows = [(m, a + b + c + d + e) for m in range(outs // 4)]
            rows.append((0, c + d + e + not_first * (a + b)))
            rows.append((0, b + c + d + e + not_first * a))
            rows.append((w // 4, a + b + c + d + not_last * e))
            rows.append((w // 4, a + b + c + not_last * (d + e)))
            for row, (m, values) in enumerate(rows):
                kept[chunks][row * ROWS : (row + 1) * ROWS, p * LANES : (p + 1) * LANES] = window(values, m)
            yield

    def average(i, kept, gold_ref):
        special = {l: outs // 4 + k for k, l in enumerate((2, 3, w, w + 1))}

        def piece(r, parity, v):
            row = (r - 2 * first_pair(v)) * ROWS
            tiles = half - 8 * v
            if tiles > 4:
                return kept[v][row : row + ROWS, parity * LANES : (parity + 1) * LANES], 0
            return kept[v][row : row + ROWS, :], parity * tiles * SLOT

        def shear(r, parity, more):
            v, slots = divmod(r // 2 + more, 8)
            value, start = piece(r, parity, v)
            if slots + SHIFT - more >= 8:
                value2, start2 = piece(r, parity, v + 1)
                if start2:
                    value2 = pltpu.roll(value2, LANES - start2, 1)
                value = jnp.where(lane8 >= slots * SLOT, value, value2)
            turn = start + slots * SLOT
            return pltpu.roll(value, LANES - turn, 1) if turn else value

        def finish(m, weight):
            values = windows(gold_ref, 2 * m + 1, slice(LANES, 2 * LANES))
            total = jnp.dot(weight, values, preferred_element_type=F32)
            for k in (0, 2):
                pair = (4 * m + k) // 2
                even, odd = total[k * ROWS : (k + 1) * ROWS], total[(k + 1) * ROWS : (k + 2) * ROWS]
                numer = jnp.where(low8, even, pltpu.roll(odd, C, 1))
                denom = jnp.where(low8, pltpu.roll(even, C, 1), odd) + outside
                value = pair_of(own_ref, i, HALO // 2 - 1 + pair) - numer / denom
                if pair == 0:
                    value = value * not_first
                if pair == outs // 2 - 1:
                    value = value * not_last
                res_ref[i, pair * SLOT + ROWS : (pair + 1) * SLOT, :] = value.astype(BF16).astype(F32)

        sheared, pairs = [], []

        def extend(count):
            for r in range(len(sheared), count):
                odd = r % 2
                sheared.append((shear(r, odd, 0), shear(r, 1 - odd, odd)))
                if r:
                    pairs.append(tuple(x + y for x, y in zip(sheared[r - 1], sheared[r])))

        for m in range(outs // 4):
            extend(4 * m + 8)
            chosen = []
            for k in range(4):
                l = 4 * m + k
                cross = [pairs[l][b] + pairs[l + 2][b] + sheared[l + 4][b] for b in range(2)]
                cross = [right(cross[k % 2], (k + 1) // 2 if k % 2 else k // 2), right(cross[1 - k % 2], k // 2)]
                mine = box_ref[i, l * ROWS : (l + 1) * ROWS, :]
                row = special.get(l, m) * ROWS
                both = []
                for p in range(2):
                    other = kept[chunks][row : row + ROWS, p * LANES : (p + 1) * LANES]
                    scale = lax.rsqrt(mine * other + 1e-05 / FACTOR**2)
                    both.append(jnp.where(valid[k][p], jnp.exp2(cross[p] * scale), 0.0))
                chosen.append(jnp.concatenate(both, 1))
            weight = jnp.concatenate(chosen, 0).astype(BF16)
            if m:
                finish(m - 1, before)
            before = weight
            yield
        finish(outs // 4 - 1, before)
        yield

    for i in range(chips):
        for x in range(outs // 2 + 1):
            res_ref[i, x * SLOT : x * SLOT + ROWS, :] = zero8
        for x in range(w // 2 + 2):
            hid_ref[i, x * SLOT : x * SLOT + ROWS, :] = zero8
    def convolve(ref, count, weight, dies):
        tiles = []
        for dy in (-1, 0, 1):
            for which in range(2):
                rows = [
                    ref[i, (p + which) * SLOT + ROWS + dy : (p + which + 1) * SLOT + dy, :]
                    for i in dies
                    for p in range(count)
                ]
                tiles.append(jnp.concatenate(rows, 0).astype(BF16))
        full = jnp.dot(jnp.concatenate(tiles, 1), weight, preferred_element_type=F32)
        return [
            (i, [full[(k * count + p) * ROWS : (k * count + p + 1) * ROWS] for p in range(count)])
            for k, i in enumerate(dies)
        ]

    def finish_dies(dies):
        for i, values in convolve(res_ref, outs // 2 - 1, weight_ref[0], dies):
            for p, value in enumerate(values):
                value = jnp.maximum(value, 0.0).astype(BF16).astype(F32)
                if p == 0:
                    value = jnp.where(low8, value * not_first, value)
                if p == w // 2:
                    value = jnp.where(low8, value, value * not_last)
                hid_ref[i, p * SLOT + ROWS : (p + 1) * SLOT, :] = value
        yield
        for i, values in convolve(hid_ref, w // 2, weight_ref[1], dies):
            for p, value in enumerate(values):
                refined[p].append(res_ref[i, (p + 1) * SLOT + ROWS : (p + 2) * SLOT, :] + value)
        yield

    refined = [[] for p in range(w // 2)]
    groups, sizes = [], [5, 3] if chips == 8 else [4] * (chips // 4)
    for size in sizes:
        groups.append(range(sum(map(len, groups)), sum(map(len, groups)) + size))
    for slot in range(chips + 5):
        running = []
        if 0 <= slot - 1 < chips:
            i = slot - 1
            running.append(products(i, kept[i % 4], golds_ref[i % 5]))
        if 0 <= slot - 4 < chips:
            i = slot - 4
            running.append(average(i, kept[i % 4], golds_ref[i % 5]))
        if slot < chips:
            running.append(stage(slot, golds_ref[slot % 5]))
        for dies in groups:
            if slot == dies[-1] + 5:
                running.append(finish_dies(dies))
        while running:
            running = [work for work in running if next(work, running) is not running]

    energy = place([jnp.concatenate(values, 0) for values in refined]) * (1.0 / C)
    sums = zero8
    for i in range(chips):
        found = energy[i * ROWS : (i + 1) * ROWS]
        out_ref[2 * i + core] = found
        mask = jnp.where(lane8 < w, pair_of(own_ref, i, cols // 2), 0.0)
        total = jnp.sum(jnp.sum(found * mask, axis=0, keepdims=True), axis=1, keepdims=True)
        count = jnp.sum(jnp.sum(mask, axis=0, keepdims=True), axis=1, keepdims=True)
        both = jnp.where(lane8 == w, total, 0.0) + jnp.where(lane8 == w + 1, count, 0.0)
        sums = sums + jnp.where(sub8 == zones[0][i], both, 0.0)
    for i in range(chips):
        for which in range(2):
            mine = jnp.sum(jnp.where(sub8 == zones[which][i], sums, 0.0), axis=0, keepdims=True)
            mine = jnp.broadcast_to(mine, (ROWS, LANES))
            if which:
                out_ref[2 * i + 1 - core] = mine
            else:
                out_ref[2 * i + core] = out_ref[2 * i + core] + mine


def score_kernel(chips, w, back_ref, out_ref):
    lane = iota((ROWS, LANES), 1)
    total = back_ref[0]
    for d in range(1, 2 * chips):
        total = total + back_ref[d]
    zone_mean = total[:, w : w + 1] / jnp.maximum(total[:, w + 1 : w + 2], 1.0)
    energy = jnp.zeros((ROWS, LANES), F32)
    for p in range(chips):
        strip = back_ref[2 * p] + back_ref[2 * p + 1]
        strip = pltpu.roll(strip, p * w, 1) if p else strip
        energy = jnp.where((lane >= p * w) & (lane < (p + 1) * w), strip, energy)
    out_ref[0] = energy / (zone_mean + 0.01)


def body(n, features, zone_ids, golden_owner, defect_mask, kernels):
    chips = n // 2
    w = defect_mask.shape[2] // chips
    cols = w + 2 * HALO
    half = cols // 2
    raw = w + 4 + 2 * REACH
    length = cols * C + LANES
    smem = pl.BlockSpec(memory_space=pltpu.SMEM)
    vmem = pl.BlockSpec(memory_space=pltpu.VMEM)
    params = pltpu.CompilerParams(vmem_limit_bytes=24 * 2**20)

    first = pl.pallas_call(
        first_kernel,
        out_shape=jax.ShapeDtypeStruct((ROWS, LANES), F32),
        out_specs=vmem,
        compiler_params=pltpu.CompilerParams(vmem_limit_bytes=2**20),
        cost_estimate=pl.CostEstimate(flops=10**9, bytes_accessed=10**6, transcendentals=0),
    )()
    packed = pl.pallas_call(
        functools.partial(pack_kernel, chips, w),
        out_shape=jax.ShapeDtypeStruct((chips, ROWS, length), BF16),
        in_specs=[smem] + [vmem] * 3,
        out_specs=vmem,
        compiler_params=params,
    )(zone_ids, first, features, defect_mask)
    groups = [[2 * p + c for p in range(chips)] for c in range(2)]
    own = lax.all_to_all(packed, "col", 0, 0, axis_index_groups=groups, tiled=True)
    other = lax.ppermute(own, "col", [(d, d ^ 1) for d in range(n)])
    tests = pl.pallas_call(
        functools.partial(test_kernel, chips, w),
        out_shape=[
            jax.ShapeDtypeStruct((chips, raw * ROWS, 4 * LANES), BF16),
            jax.ShapeDtypeStruct((chips, (w + 4) * ROWS, LANES), F32),
        ],
        in_specs=[vmem],
        out_specs=[vmem] * 2,
        scratch_shapes=[
            pltpu.VMEM((chips * (raw // 2) * ROWS, 2 * LANES), F32),
        ]
        + [pltpu.VMEM((raw * SLOT + ROWS, LANES), F32)] * 6
        + [pltpu.VMEM(((w + 4) * SLOT + ROWS, LANES), F32)] * 2,
        compiler_params=params,
        cost_estimate=pl.CostEstimate(flops=10**9, bytes_accessed=10**6, transcendentals=0),
    )(own)
    weights = pl.pallas_call(
        weight_kernel,
        out_shape=jax.ShapeDtypeStruct((2, 12 * C, LANES), BF16),
        in_specs=[vmem],
        out_specs=vmem,
        compiler_params=params,
        cost_estimate=pl.CostEstimate(flops=10**8, bytes_accessed=10**6, transcendentals=0),
    )(jnp.swapaxes(kernels, 1, 2))
    me = lax.axis_index("col").astype(jnp.int32).reshape(1)
    chunks = -(-half // 8)
    reach = [min(raw // 2, 8 * v + 8) - max(0, 8 * v - SHIFT) for v in range(chunks)]
    kept = [
        pltpu.VMEM((2 * reach[v] * ROWS, (2 if half - 8 * v > 4 else 1) * LANES), F32) for v in range(chunks)
    ] + [pltpu.VMEM(((w // 4 + 5) * ROWS, 2 * LANES), F32)]
    rows = half * SLOT + -(-half // 8) * LANES
    partial = pl.pallas_call(
        functools.partial(main_kernel, chips, w),
        out_shape=jax.ShapeDtypeStruct((n, ROWS, LANES), F32),
        in_specs=[smem, smem] + [vmem] * 5,
        out_specs=vmem,
        scratch_shapes=[
            pltpu.VMEM((chips, (w // 2 + 2) * SLOT + ROWS, LANES), F32),
            pltpu.VMEM((chips, (w // 2 + 1) * SLOT + ROWS, LANES), F32),
        ]
        + [pltpu.VMEM((cols * SLOT, LANES), F32)] * 4
        + [pltpu.VMEM((rows, 4 * LANES), BF16)] * 5
        + kept * 4,
        compiler_params=params,
    )(me, golden_owner, own, other, *tests, weights)
    back = lax.all_to_all(partial, "col", 0, 0, tiled=True)
    return pl.pallas_call(
        functools.partial(score_kernel, chips, w),
        out_shape=jax.ShapeDtypeStruct(defect_mask.shape, F32),
        in_specs=[vmem],
        out_specs=vmem,
        compiler_params=params,
    )(back)


def solution(mesh):
    split = P(("groups", "col"), None, None)
    return jax.shard_map(
        functools.partial(body, mesh.shape["col"]),
        mesh=mesh,
        in_specs=(split, P(("groups", "col")), P("groups"), split, P()),
        out_specs=split,
        check_vma=False,
    )
```

```python
import functools

import jax
import jax.numpy as jnp
from jax import lax
from jax.experimental import pallas as pl
from jax.experimental.pallas import tpu as pltpu
from jax.sharding import PartitionSpec as P

C = 64
SHIFT = 6
BOX = 5
Z = 8
SIDE = 2 * SHIFT + 1
REACH = BOX // 2
HALO = SHIFT + REACH + 2
ROWS = 8
SLOT = 16
TOP = (SLOT - ROWS) // 2
LANES = 128
FACTOR = 32.0 * 1.4426950408889634
F32 = jnp.float32
BF16 = jnp.bfloat16


def iota(shape, dim):
    return lax.broadcasted_iota(jnp.int32, shape, dim)


def first_kernel(out_ref):
    out_ref[...] = jnp.zeros((ROWS, LANES), F32)


def pack_kernel(chips, w, zone_ref, first_ref, feat_ref, mask_ref, out_ref):
    cols = w + 2 * HALO
    width = mask_ref.shape[2]
    mask = mask_ref[0].astype(F32)
    zone = first_ref[...] + zone_ref[0].astype(F32)
    lane = iota((ROWS, LANES), 1)
    for p in range(chips):
        for t in range(cols // 2):
            col = p * w - HALO + 2 * t
            at = slice(t * LANES, (t + 1) * LANES)
            if 0 <= col < width:
                out_ref[p, :, at] = feat_ref[0, :, col * C : (col + 2) * C]
            else:
                out_ref[p, :, at] = jnp.zeros((ROWS, LANES), BF16)
        here = pltpu.roll(mask, (width - p * w) % width, 1) if p else mask
        out_ref[p, :, cols * C :] = jnp.where(lane < w, here, zone).astype(BF16)


def pair_of(ref, i, t):
    return ref[i, :, t * LANES : (t + 1) * LANES].astype(F32)


def split_square(values):
    square = values * values
    high = square.astype(BF16).astype(F32)
    return high, square - high


def place(values):
    row, col = iota((LANES, LANES), 0), iota((LANES, LANES), 1)
    highs, lows = zip(*(split_square(value) for value in values))
    squares = [jnp.concatenate([part.astype(BF16) for part in parts], 1) for parts in (highs, lows)]
    picks = [(col == 2 * q + row // C).astype(BF16) for q in range(len(values))]
    sums = jnp.dot(jnp.concatenate(squares, 0), jnp.concatenate(picks, 0), preferred_element_type=F32)
    rows = sums.shape[0] // 2
    return sums[:rows] + sums[rows:]


def test_kernel(chips, w, own_ref, test_ref, box_ref, wide_ref, *scratch):
    raw = w + 4 + 2 * REACH
    before = HALO - REACH - 2
    zero8 = jnp.zeros((ROWS, LANES), F32)
    lo, hi = slice(0, C), slice(C, LANES)

    for ref in scratch:
        for i in range(0, ref.shape[0], ROWS):
            ref[i : i + ROWS, :] = zero8
    pairs = []
    for t in range(before // 2, (before + raw) // 2):
        pairs.append([pair_of(own_ref, i, t) for i in range(chips)])
    parts = [split_square(jnp.concatenate([tiles[i] for tiles in pairs], 0)) for i in range(chips)]
    squares = [jnp.concatenate([part[k].astype(BF16) for part in parts], 0) for k in range(2)]
    both = (iota((2 * LANES, 2 * LANES), 0) % LANES // C == iota((2 * LANES, 2 * LANES), 1) // LANES).astype(BF16)
    wide_ref[...] = jnp.dot(jnp.concatenate(squares, 1), both, preferred_element_type=F32)
    scale = 1.0 / FACTOR**2
    for i in range(chips):
        energy = []
        for r in range(raw):
            row = (i * (raw // 2) + r // 2) * ROWS
            energy.append(wide_ref[row : row + ROWS, r % 2 * LANES : (r % 2 + 1) * LANES])
        twos = [x + y for x, y in zip(energy, energy[1:])]
        ref = scratch[6 + i % 2]
        for l in range(w + 4):
            ref[l * SLOT + ROWS : (l + 1) * SLOT, :] = (twos[l] + twos[l + 2] + energy[l + 4]) * scale
        for l in range(w + 4):
            base = l * SLOT + ROWS
            rows = [ref[base + dy : base + dy + ROWS, :] for dy in range(-2, 3)]
            box_ref[i, l * ROWS : (l + 1) * ROWS, :] = sum(rows[1:], rows[0])

    for i in range(chips):
        refs = scratch[3 * (i % 2) : 3 * (i % 2) + 3]
        for q in range(raw // 2):
            here = pairs[q][i]
            turned = pltpu.roll(here, C, 1)
            for odd, (left, right) in enumerate(((here, turned), (turned, here))):
                top = (2 * q + odd) * SLOT + ROWS
                refs[0][top + 2 : top + 2 + ROWS, lo] = left[:, lo]
                refs[0][top + 1 : top + 1 + ROWS, hi] = right[:, hi]
                refs[1][top : top + ROWS, lo] = left[:, lo]
                refs[2][top - 1 : top - 1 + ROWS, lo] = left[:, lo]
                refs[2][top - 2 : top - 2 + ROWS, hi] = right[:, hi]
        for r in range(0, raw, 2):
            at = slice(r * ROWS, (r + 2) * ROWS)
            for t, ref in enumerate(refs):
                two = [ref[q * SLOT + ROWS : (q + 1) * SLOT, :] for q in (r, r + 1)]
                test_ref[i, at, t * LANES : (t + 1) * LANES] = jnp.concatenate(two, 0).astype(BF16)
            test_ref[i, at, 3 * LANES :] = jnp.zeros((2 * ROWS, LANES), BF16)


def weight_kernel(kern_ref, weight_ref):
    twice = (iota((C, LANES), 1) % C == iota((C, LANES), 0)).astype(BF16)
    low = iota((C, LANES), 1) < C
    for conv in range(2):
        doubled = lax.dot_general(kern_ref[conv], twice, (((0,), (0,)), ((), ())), preferred_element_type=F32)
        for dy in range(3):
            for at in range(4):
                taps = [
                    doubled[(3 * dy + dx) * C : (3 * dy + dx + 1) * C] if 0 <= dx < 3 else jnp.zeros((C, LANES), F32)
                    for dx in (at, at - 1)
                ]
                row = (4 * dy + at) * C
                weight_ref[conv, row : row + C, :] = jnp.where(low, taps[0], taps[1]).astype(BF16)


def main_kernel(
    chips, w, me_ref, owner_ref, own_ref, other_ref, test_ref, box_ref, weight_ref, out_ref,
    res_ref, hid_ref, g0_ref, g1_ref, g2_ref, gsq_ref, *scratch
):
    cols = w + 2 * HALO
    half = cols // 2
    raw = w + 4 + 2 * REACH
    outs = w + 4
    odds = half * SLOT
    chunks = -(-half // 8)
    lanes_g = chunks * LANES
    golds_ref = scratch[:5]
    kept = [scratch[5 + k * (chunks + 1) : 5 + (k + 1) * (chunks + 1)] for k in range(4)]
    me = me_ref[0]
    chip = me // 2
    core = me % 2
    not_first = jnp.where(chip == 0, 0.0, 1.0).astype(F32)
    not_last = jnp.where(chip == chips - 1, 0.0, 1.0).astype(F32)

    lane8 = iota((ROWS, LANES), 1)
    sub8 = iota((ROWS, LANES), 0)
    low8 = lane8 < C
    zero8 = jnp.zeros((ROWS, LANES), F32)
    lo = slice(0, C)
    hi = slice(C, LANES)

    zones = [
        [pair_of(ref, i, cols // 2)[0, w].astype(jnp.int32) for i in range(chips)] for ref in (own_ref, other_ref)
    ]
    golds = [owner_ref[zone] for zone in zones[0]]

    for ref in (g0_ref, g1_ref, g2_ref, gsq_ref):
        for i in range(0, ref.shape[0], ROWS):
            ref[i : i + ROWS, :] = jnp.where(low8, 0.0, 1.0) if ref is g1_ref else zero8
    if half % 8 > 4:
        for ref in golds_ref:
            ref[cols * SLOT :, :] = jnp.zeros((ref.shape[0] - cols * SLOT, 4 * LANES), BF16)
    summing = (iota((SLOT, 4 * LANES), 1) >= 3 * LANES).astype(BF16)

    valid = []
    for k in range(4):
        a = lane8 % SLOT - TOP - sub8
        both = []
        for parity in range(2):
            b = lane8 // SLOT * 2 + parity - k
            both.append((b >= 0) & (b < SIDE) & (jnp.abs(a) <= SHIFT))
        valid.append(both)
    outside = jnp.maximum(SHIFT - TOP - sub8, 0) + jnp.maximum(sub8 + SHIFT - (SLOT - TOP - 1), 0)
    outside = (outside * SIDE).astype(F32)

    def stage(i, gold_ref):
        owner = golds[i]
        mine = owner % 2 == core
        for t in range(cols // 2):
            here = jnp.where(mine, pair_of(own_ref, owner // 2, t), pair_of(other_ref, owner // 2, t))
            turned = pltpu.roll(here, C, 1)
            for odd, (left, right) in enumerate(((here, turned), (turned, here))):
                top = odd * odds + t * SLOT + TOP
                g0_ref[top + 2 : top + 2 + ROWS, lo] = left[:, lo]
                g0_ref[top + 1 : top + 1 + ROWS, hi] = right[:, hi]
                g1_ref[top : top + ROWS, lo] = left[:, lo]
                g2_ref[top - 1 : top - 1 + ROWS, lo] = left[:, lo]
                g2_ref[top - 2 : top - 2 + ROWS, hi] = right[:, hi]
                high, low = split_square(jnp.where(low8, left, right))
                gsq_ref[top : top + ROWS, :] = jnp.where(low8, high, low)
            yield
        for parity in range(2):
            for g in range(half):
                at = slice(parity * odds + g * SLOT, parity * odds + (g + 1) * SLOT)
                for t, ref in enumerate((g0_ref, g1_ref, g2_ref, gsq_ref)):
                    gold_ref[at, t * LANES : (t + 1) * LANES] = ref[at, :].astype(BF16)
                if g % 6 == 5:
                    yield

    def right(value, slots):
        return pltpu.roll(value, slots * SLOT, 1) if slots else value

    def windows(gold_ref, tile, at):
        rows = [slice(p * odds + tile * SLOT, p * odds + (tile + 8) * SLOT) for p in range(2)]
        return jnp.concatenate([gold_ref[rows[0], at], gold_ref[rows[1], at]], 0)

    def first_pair(v):
        return max(0, 8 * v - SHIFT)

    def products(i, kept, gold_ref):
        energies = ([], [])
        for v in range(chunks):
            first, last = first_pair(v), min(raw // 2 - 1, 8 * v + 7)
            tiles = min(8, half - 8 * v)
            rows = [slice(p * odds + 8 * v * SLOT, p * odds + (8 * v + (tiles if tiles <= 4 else 8)) * SLOT) for p in range(2)]
            parts = [gold_ref[rows[0], :], gold_ref[rows[1], :]]
            if tiles < 4:
                parts.append(gold_ref[: (8 - 2 * tiles) * SLOT, :])
            block = lax.dot_general(
                jnp.concatenate([summing, test_ref[i, 2 * first * ROWS : 2 * (last + 1) * ROWS, :]], 0),
                jnp.concatenate(parts, 0),
                (((1,), (1,)), ((), ())),
                preferred_element_type=F32,
            )
            for p in range(2):
                at = slice(p * LANES, (p + 1) * LANES) if tiles > 4 else slice(0, LANES)
                start = 0 if tiles > 4 else p * tiles * SLOT
                here = block[:ROWS, at]
                energies[p].append(pltpu.roll(here, LANES - start, 1) if start else here)
            kept[v][...] = block[SLOT:]
            yield

        by_parity = []
        for parity in range(2):
            parts = []
            for here in energies[parity]:
                down = here
                for dy in (-2, -1, 1, 2):
                    inside = (sub8 + dy >= 0) & (sub8 + dy < ROWS)
                    down = down + jnp.where(inside, pltpu.roll(here, (-dy) % LANES, 1), 0.0)
                parts.append(down)
            by_parity.append(jnp.concatenate(parts, 1))
        even, odd = by_parity
        even1, even2 = (pltpu.roll(even, lanes_g - d * SLOT, 1) for d in (1, 2))
        odd1, odd2 = (pltpu.roll(odd, lanes_g - d * SLOT, 1) for d in (1, 2))
        def window(values, m):
            v, offset = divmod(2 * m * SLOT, LANES)
            first = values[:, v * LANES : (v + 1) * LANES]
            if not offset:
                return first
            second = values[:, (v + 1) * LANES : (v + 2) * LANES]
            return pltpu.roll(jnp.where(lane8 >= offset, first, second), LANES - offset, 1)

        for p, terms in enumerate(((even, odd, even1, odd1, even2), (odd, even1, odd1, even2, odd2))):
            a, b, c, d, e = terms
            rows = [(m, a + b + c + d + e) for m in range(outs // 4)]
            rows.append((0, c + d + e + not_first * (a + b)))
            rows.append((0, b + c + d + e + not_first * a))
            rows.append((w // 4, a + b + c + d + not_last * e))
            rows.append((w // 4, a + b + c + not_last * (d + e)))
            for row, (m, values) in enumerate(rows):
                kept[chunks][row * ROWS : (row + 1) * ROWS, p * LANES : (p + 1) * LANES] = window(values, m)
            yield

    def average(i, kept, gold_ref):
        special = {l: outs // 4 + k for k, l in enumerate((2, 3, w, w + 1))}

        def piece(r, parity, v):
            row = (r - 2 * first_pair(v)) * ROWS
            tiles = half - 8 * v
            if tiles > 4:
                return kept[v][row : row + ROWS, parity * LANES : (parity + 1) * LANES], 0
            return kept[v][row : row + ROWS, :], parity * tiles * SLOT

        def shear(r, parity, more):
            v, slots = divmod(r // 2 + more, 8)
            value, start = piece(r, parity, v)
            if slots + SHIFT - more >= 8:
                value2, start2 = piece(r, parity, v + 1)
                if start2:
                    value2 = pltpu.roll(value2, LANES - start2, 1)
                value = jnp.where(lane8 >= slots * SLOT, value, value2)
            turn = start + slots * SLOT
            return pltpu.roll(value, LANES - turn, 1) if turn else value

        def finish(m, weight):
            values = windows(gold_ref, 2 * m + 1, slice(LANES, 2 * LANES))
            total = jnp.dot(weight, values, preferred_element_type=F32)
            for k in (0, 2):
                pair = (4 * m + k) // 2
                even, odd = total[k * ROWS : (k + 1) * ROWS], total[(k + 1) * ROWS : (k + 2) * ROWS]
                numer = jnp.where(low8, even, pltpu.roll(odd, C, 1))
                denom = jnp.where(low8, pltpu.roll(even, C, 1), odd) + outside
                value = pair_of(own_ref, i, HALO // 2 - 1 + pair) - numer / denom
                if pair == 0:
                    value = value * not_first
                if pair == outs // 2 - 1:
                    value = value * not_last
                res_ref[i, pair * SLOT + ROWS : (pair + 1) * SLOT, :] = value.astype(BF16).astype(F32)

        sheared, pairs = [], []

        def extend(count):
            for r in range(len(sheared), count):
                odd = r % 2
                sheared.append((shear(r, odd, 0), shear(r, 1 - odd, odd)))
                if r:
                    pairs.append(tuple(x + y for x, y in zip(sheared[r - 1], sheared[r])))

        for m in range(outs // 4):
            extend(4 * m + 8)
            chosen = []
            for k in range(4):
                l = 4 * m + k
                cross = [pairs[l][b] + pairs[l + 2][b] + sheared[l + 4][b] for b in range(2)]
                cross = [right(cross[k % 2], (k + 1) // 2 if k % 2 else k // 2), right(cross[1 - k % 2], k // 2)]
                mine = box_ref[i, l * ROWS : (l + 1) * ROWS, :]
                row = special.get(l, m) * ROWS
                both = []
                for p in range(2):
                    other = kept[chunks][row : row + ROWS, p * LANES : (p + 1) * LANES]
                    scale = lax.rsqrt(mine * other + 1e-05 / FACTOR**2)
                    both.append(jnp.where(valid[k][p], jnp.exp2(cross[p] * scale), 0.0))
                chosen.append(jnp.concatenate(both, 1))
            weight = jnp.concatenate(chosen, 0).astype(BF16)
            if m:
                finish(m - 1, before)
            before = weight
            yield
        finish(outs // 4 - 1, before)
        yield

    for i in range(chips):
        for x in range(outs // 2 + 1):
            res_ref[i, x * SLOT : x * SLOT + ROWS, :] = zero8
        for x in range(w // 2 + 2):
            hid_ref[i, x * SLOT : x * SLOT + ROWS, :] = zero8
    def convolve(ref, count, weight, dies):
        tiles = []
        for dy in (-1, 0, 1):
            for which in range(2):
                rows = [
                    ref[i, (p + which) * SLOT + ROWS + dy : (p + which + 1) * SLOT + dy, :]
                    for i in dies
                    for p in range(count)
                ]
                tiles.append(jnp.concatenate(rows, 0).astype(BF16))
        full = jnp.dot(jnp.concatenate(tiles, 1), weight, preferred_element_type=F32)
        return [
            (i, [full[(k * count + p) * ROWS : (k * count + p + 1) * ROWS] for p in range(count)])
            for k, i in enumerate(dies)
        ]

    def finish_dies(dies):
        for i, values in convolve(res_ref, outs // 2 - 1, weight_ref[0], dies):
            for p, value in enumerate(values):
                value = jnp.maximum(value, 0.0).astype(BF16).astype(F32)
                if p == 0:
                    value = jnp.where(low8, value * not_first, value)
                if p == w // 2:
                    value = jnp.where(low8, value, value * not_last)
                hid_ref[i, p * SLOT + ROWS : (p + 1) * SLOT, :] = value
        yield
        for i, values in convolve(hid_ref, w // 2, weight_ref[1], dies):
            for p, value in enumerate(values):
                refined[p].append(res_ref[i, (p + 1) * SLOT + ROWS : (p + 2) * SLOT, :] + value)
        yield

    refined = [[] for p in range(w // 2)]
    groups, sizes = [], [5, 3] if chips == 8 else [4] * (chips // 4)
    for size in sizes:
        groups.append(range(sum(map(len, groups)), sum(map(len, groups)) + size))
    for slot in range(chips + 5):
        running = []
        if 0 <= slot - 1 < chips:
            i = slot - 1
            running.append(products(i, kept[i % 4], golds_ref[i % 5]))
        if 0 <= slot - 4 < chips:
            i = slot - 4
            running.append(average(i, kept[i % 4], golds_ref[i % 5]))
        if slot < chips:
            running.append(stage(slot, golds_ref[slot % 5]))
        for dies in groups:
            if slot == dies[-1] + 5:
                running.append(finish_dies(dies))
        while running:
            running = [work for work in running if next(work, running) is not running]

    energy = place([jnp.concatenate(values, 0) for values in refined]) * (1.0 / C)
    sums = zero8
    for i in range(chips):
        found = energy[i * ROWS : (i + 1) * ROWS]
        line = jnp.sum(pltpu.roll(found, 0, 1, stride=w, stride_axis=0), axis=0, keepdims=True)
        out_ref[2 * i + core, 0:1, :] = line
        out_ref[2 * i + 1 - core, 0:1, :] = zero8[:1]
        mask = jnp.where(lane8 < w, pair_of(own_ref, i, cols // 2), 0.0)
        total = jnp.sum(jnp.sum(found * mask, axis=0, keepdims=True), axis=1, keepdims=True)
        count = jnp.sum(jnp.sum(mask, axis=0, keepdims=True), axis=1, keepdims=True)
        both = jnp.where(lane8 == w, total, 0.0) + jnp.where(lane8 == w + 1, count, 0.0)
        sums = sums + jnp.where(sub8 == zones[0][i], both, 0.0)
    for i in range(chips):
        for which in range(2):
            mine = jnp.sum(jnp.where(sub8 == zones[which][i], sums, 0.0), axis=0, keepdims=True)
            out_ref[2 * i + (1 - core if which else core), 1:2, :] = mine


def score_kernel(chips, w, back_ref, out_ref):
    lane, sub = iota((ROWS, LANES), 1), iota((ROWS, LANES), 0)
    total = back_ref[0, 1:2, :]
    for d in range(1, 2 * chips):
        total = total + back_ref[d, 1:2, :]
    zone_mean = total[:, w : w + 1] / jnp.maximum(total[:, w + 1 : w + 2], 1.0)
    energy = jnp.zeros((ROWS, LANES), F32)
    for p in range(chips):
        line = back_ref[2 * p, 0:1, :] + back_ref[2 * p + 1, 0:1, :]
        strip = jnp.broadcast_to(line, (ROWS, LANES))
        strip = pltpu.roll(strip, p * w, 1) if p else strip
        for bit in (1, 2, 4):
            strip = jnp.where(sub & bit != 0, pltpu.roll(strip, LANES - bit * w, 1), strip)
        energy = jnp.where((lane >= p * w) & (lane < (p + 1) * w), strip, energy)
    out_ref[0] = energy / (zone_mean + 0.01)


def body(n, features, zone_ids, golden_owner, defect_mask, kernels):
    chips = n // 2
    w = defect_mask.shape[2] // chips
    cols = w + 2 * HALO
    half = cols // 2
    raw = w + 4 + 2 * REACH
    length = cols * C + LANES
    smem = pl.BlockSpec(memory_space=pltpu.SMEM)
    vmem = pl.BlockSpec(memory_space=pltpu.VMEM)
    params = pltpu.CompilerParams(vmem_limit_bytes=24 * 2**20)

    first = pl.pallas_call(
        first_kernel,
        out_shape=jax.ShapeDtypeStruct((ROWS, LANES), F32),
        out_specs=vmem,
        compiler_params=pltpu.CompilerParams(vmem_limit_bytes=2**20),
        cost_estimate=pl.CostEstimate(flops=10**9, bytes_accessed=10**6, transcendentals=0),
    )()
    packed = pl.pallas_call(
        functools.partial(pack_kernel, chips, w),
        out_shape=jax.ShapeDtypeStruct((chips, ROWS, length), BF16),
        in_specs=[smem] + [vmem] * 3,
        out_specs=vmem,
        compiler_params=params,
    )(zone_ids, first, features, defect_mask)
    groups = [[2 * p + c for p in range(chips)] for c in range(2)]
    own = lax.all_to_all(packed, "col", 0, 0, axis_index_groups=groups, tiled=True)
    other = lax.ppermute(own, "col", [(d, d ^ 1) for d in range(n)])
    tests = pl.pallas_call(
        functools.partial(test_kernel, chips, w),
        out_shape=[
            jax.ShapeDtypeStruct((chips, raw * ROWS, 4 * LANES), BF16),
            jax.ShapeDtypeStruct((chips, (w + 4) * ROWS, LANES), F32),
        ],
        in_specs=[vmem],
        out_specs=[vmem] * 2,
        scratch_shapes=[
            pltpu.VMEM((chips * (raw // 2) * ROWS, 2 * LANES), F32),
        ]
        + [pltpu.VMEM((raw * SLOT + ROWS, LANES), F32)] * 6
        + [pltpu.VMEM(((w + 4) * SLOT + ROWS, LANES), F32)] * 2,
        compiler_params=params,
        cost_estimate=pl.CostEstimate(flops=10**9, bytes_accessed=10**6, transcendentals=0),
    )(own)
    weights = pl.pallas_call(
        weight_kernel,
        out_shape=jax.ShapeDtypeStruct((2, 12 * C, LANES), BF16),
        in_specs=[vmem],
        out_specs=vmem,
        compiler_params=params,
        cost_estimate=pl.CostEstimate(flops=10**8, bytes_accessed=10**6, transcendentals=0),
    )(jnp.swapaxes(kernels, 1, 2))
    me = lax.axis_index("col").astype(jnp.int32).reshape(1)
    chunks = -(-half // 8)
    reach = [min(raw // 2, 8 * v + 8) - max(0, 8 * v - SHIFT) for v in range(chunks)]
    kept = [
        pltpu.VMEM((2 * reach[v] * ROWS, (2 if half - 8 * v > 4 else 1) * LANES), F32) for v in range(chunks)
    ] + [pltpu.VMEM(((w // 4 + 5) * ROWS, 2 * LANES), F32)]
    rows = half * SLOT + -(-half // 8) * LANES
    partial = pl.pallas_call(
        functools.partial(main_kernel, chips, w),
        out_shape=jax.ShapeDtypeStruct((n, 2, LANES), F32),
        in_specs=[smem, smem] + [vmem] * 5,
        out_specs=vmem,
        scratch_shapes=[
            pltpu.VMEM((chips, (w // 2 + 2) * SLOT + ROWS, LANES), F32),
            pltpu.VMEM((chips, (w // 2 + 1) * SLOT + ROWS, LANES), F32),
        ]
        + [pltpu.VMEM((cols * SLOT, LANES), F32)] * 4
        + [pltpu.VMEM((rows, 4 * LANES), BF16)] * 5
        + kept * 4,
        compiler_params=params,
    )(me, golden_owner, own, other, *tests, weights)
    back = lax.all_to_all(partial, "col", 0, 0, tiled=True)
    return pl.pallas_call(
        functools.partial(score_kernel, chips, w),
        out_shape=jax.ShapeDtypeStruct(defect_mask.shape, F32),
        in_specs=[vmem],
        out_specs=vmem,
        compiler_params=params,
    )(back)


def solution(mesh):
    split = P(("groups", "col"), None, None)
    return jax.shard_map(
        functools.partial(body, mesh.shape["col"]),
        mesh=mesh,
        in_specs=(split, P(("groups", "col")), P("groups"), split, P()),
        out_specs=split,
        check_vma=False,
    )
```
